128 devices in a mesh: grid: 8 (over x, core), dom: 16 (over z, y).
Axes of the slice: x: 4, y: 4, z: 4, core: 2. Of those that a mesh axis runs over, the one named last changes fastest.
Arguments:
- grid_features: bfloat16 [8, 16, 512, 474], P('grid', 'dom'), may hold values from -6 to 6
- mesh_latent: bfloat16 [8, 16, 256, 512], P('grid', 'dom'), may hold values from -6 to 6
- encode_edges: bfloat16 [8, 16, 1024, 512], P('grid', 'dom'), may hold values from -6 to 6
- encode_senders: int32 [8, 16, 1024], P('grid', 'dom'), may hold values from 448 to 4159, as said below
- encode_targets: int32 [8, 16, 1024], P('grid', 'dom'), may hold values from 0 to 256, as said below
- mesh_edges: bfloat16 [8, 16, 2048, 512], P('grid', 'dom'), may hold values from -6 to 6
- mesh_senders: int32 [8, 16, 2048], P('grid', 'dom'), may hold values from 224 to 4351, as said below
- mesh_targets: int32 [8, 16, 2048], P('grid', 'dom'), may hold values from 0 to 255
- decode_edges: bfloat16 [8, 16, 1536, 512], P('grid', 'dom'), may hold values from -6 to 6
- decode_senders: int32 [8, 16, 1536], P('grid', 'dom'), may hold values from 224 to 2079, as said below
- embed_first: bfloat16 [474, 512], replicated, may hold values from -0.25 to 0.25
- embed_second: bfloat16 [512, 512], replicated, may hold values from -0.25 to 0.25
- embed_gain: float32 [512], replicated, may hold values from 0.1 to 1.9
- encode_weights: bfloat16 [7, 512, 512], replicated, may hold values from -0.25 to 0.25
- encode_gains: float32 [2, 512], replicated, may hold values from 0.1 to 1.9
- mesh_weights: bfloat16 [2, 7, 512, 512], replicated, may hold values from -0.25 to 0.25
- mesh_gains: float32 [2, 2, 512], replicated, may hold values from 0.1 to 1.9
- decode_weights: bfloat16 [7, 512, 512], replicated, may hold values from -0.25 to 0.25
- decode_gains: float32 [2, 512], replicated, may hold values from 0.1 to 1.9
Outputs:
- grid_out: bfloat16 [8, 16, 512, 512], P('grid', 'dom')
- mesh_out: bfloat16 [8, 16, 256, 512], P('grid', 'dom')
The draws below stay inside these ranges and needn't reach their ends.
Inputs may be any that keep to these rules, and one draw needn't show every extreme that they name: `encode_senders`: each value is r * 512 + q with r = 3 (i + 1) + j + 1 naming the block nbr offset (i, j), never a block outside the grid of partitions; for r = 4 q is any row, for r under 4 q is one of the last 64 rows of the block, for r over 4 one of the first 64. `encode_targets`: the value 256 marks an empty slot; the partitions of the first and last band fill all 1024 slots, the others the first half. `mesh_senders`: values under 9 * 256 name a neighbourhood row as for the encoder, with 256 rows a block and 32 in place of 64; larger values name row v - 2304 of the coarse table. `decode_senders`: each value names a neighbourhood row as for the encoder, with 256 rows a block and 32 in place of 64.
All inputs are finite; a program needn't handle non-finite values.
Results may differ from the reference program's by a relative error of at most 0.02.
Values may be sent and summed in bfloat16 or wider, within the bound.
A program may use at most 128 MiB of HBM per device.

```python
import jax
import jax.numpy as jnp
from jax import lax

L = 512
C_IN = 474
G_DEV = 512
M_DEV = 256
COARSE_DEV = 16
RIM_G = 64
RIM_M = 32
LAYERS = 2
ENC_DEV = 1024
MESH_EDGES_DEV = 2048
N_GRID = 8
N_DOM = 16


def neighbour_rows(key, slot_count, row_count, rim_count):
    subkeys = jax.random.split(key, 5)
    array_shape = (N_GRID, N_DOM, slot_count)
    band_index = jnp.arange(N_GRID, dtype=jnp.int32)[:, None, None]
    sector_index = jnp.arange(N_DOM, dtype=jnp.int32)[None, :, None]
    band_step = jax.random.randint(subkeys[0], array_shape, -1, 2)
    sector_step = jax.random.randint(subkeys[1], array_shape, -1, 2)
    staying = jax.random.randint(subkeys[2], array_shape, 0, 2)
    band_step = jnp.where((staying == 1) | (band_index + band_step < 0) | (band_index + band_step >= N_GRID), 0, band_step)
    sector_step = jnp.where((staying == 1) | (sector_index + sector_step < 0) | (sector_index + sector_step >= N_DOM), 0, sector_step)
    offset_code = (band_step + 1) * 3 + sector_step + 1
    anywhere = jax.random.randint(subkeys[3], array_shape, 0, row_count)
    facing = jax.random.randint(subkeys[4], array_shape, 0, rim_count)
    row_pick = jnp.where(offset_code == 4, anywhere, jnp.where(offset_code < 4, row_count - rim_count + facing, facing))
    return (offset_code * row_count + row_pick).astype(jnp.int32)


def draw_encode_senders(key, part):
    key = jax.random.fold_in(key, 11)
    return neighbour_rows(key, ENC_DEV, G_DEV, RIM_G)


def draw_encode_targets(key, part):
    key = jax.random.fold_in(key, 12)
    array_shape = (N_GRID, N_DOM, ENC_DEV)
    band_index = jnp.arange(N_GRID, dtype=jnp.int32)[:, None, None]
    slot_index = jnp.arange(ENC_DEV, dtype=jnp.int32)[None, None, :]
    live_count = jnp.where((band_index == 0) | (band_index == N_GRID - 1), ENC_DEV, ENC_DEV // 2)
    picks = jax.random.randint(key, array_shape, 0, M_DEV)
    return jnp.where(slot_index < live_count, picks, M_DEV).astype(jnp.int32)


def draw_mesh_senders(key, part):
    key = jax.random.fold_in(key, 13)
    subkeys = jax.random.split(key, 3)
    array_shape = (N_GRID, N_DOM, MESH_EDGES_DEV)
    nearby = neighbour_rows(subkeys[0], MESH_EDGES_DEV, M_DEV, RIM_M)
    distant = 9 * M_DEV + jax.random.randint(subkeys[1], array_shape, 0, COARSE_DEV * N_GRID * N_DOM)
    choose = jax.random.randint(subkeys[2], array_shape, 0, 4)
    return jnp.where(choose == 0, distant, nearby).astype(jnp.int32)


def draw_decode_senders(key, part):
    key = jax.random.fold_in(key, 14)
    return neighbour_rows(key, 3 * G_DEV, M_DEV, RIM_M)


def place_ends(values, own_key, least, top_value):
    shape = values.shape
    place = [jax.random.randint(jax.random.fold_in(own_key, axis), (), 0, shape[axis]) for axis in range(len(shape))]
    values = values.at[tuple(place)].set(least)
    longest = shape.index(max(shape))
    place[longest] = (place[longest] + 1) % shape[longest]
    return values.at[tuple(place)].set(top_value)


def shard_levels(key, extent, shards, least, top_value):
    def one(position, shards_of):
        steps = jax.random.uniform(jax.random.fold_in(jax.random.fold_in(key, 6), position), (shards_of,), jnp.float32, least / len(shards), top_value / len(shards))
        return jnp.repeat(jnp.exp(steps), extent[position] // shards_of).reshape((-1,) + (1,) * (len(extent) - position - 1))

    level = one(*shards[0])
    for cut in shards[1:]:
        level = level * one(*cut)
    return level


def scatter_about(rng, extent, scale, bound, shards=(), kind=jnp.bfloat16):
    result = jax.random.normal(rng, extent, jnp.float32) * scale
    if len(shards) > 0:
        result = shard_levels(rng, extent, shards, -0.22, 0.18) * result
    return jnp.clip(result, min=-bound, max=bound).astype(kind)


def setup_inputs(seed: int = 0) -> dict:
    keys = jax.random.split(jax.random.key(seed), 20)
    grid_features = scatter_about(keys[0], (N_GRID, N_DOM, G_DEV, C_IN), 1.0, 6.0, ((0, 8), (1, 16)))
    mesh_latent = scatter_about(keys[1], (N_GRID, N_DOM, M_DEV, L), 1.0, 6.0, ((0, 8), (1, 16)))
    encode_edges = scatter_about(keys[2], (N_GRID, N_DOM, ENC_DEV, L), 1.0, 6.0, ((0, 8), (1, 16)))
    encode_senders = draw_encode_senders(jax.random.fold_in(keys[19], 71), 0)
    encode_targets = draw_encode_targets(jax.random.fold_in(keys[19], 71), 0)
    mesh_edges = scatter_about(keys[5], (N_GRID, N_DOM, MESH_EDGES_DEV, L), 1.0, 6.0, ((0, 8), (1, 16)))
    mesh_senders = draw_mesh_senders(jax.random.fold_in(keys[19], 71), 0)
    mesh_targets = place_ends(jax.random.randint(keys[7], (N_GRID, N_DOM, MESH_EDGES_DEV), 0, M_DEV), jax.random.fold_in(keys[7], 1), 0, M_DEV - 1).astype(jnp.int32)
    decode_edges = scatter_about(keys[8], (N_GRID, N_DOM, 3 * G_DEV, L), 1.0, 6.0, ((0, 8), (1, 16)))
    decode_senders = draw_decode_senders(jax.random.fold_in(keys[19], 71), 0)
    embed_first = scatter_about(keys[10], (C_IN, L), C_IN ** -0.5, 0.25)
    embed_second = scatter_about(keys[11], (L, L), L ** -0.5, 0.25)
    embed_gain = jnp.clip(1.0 + 0.18 * jax.random.normal(keys[12], (L,), jnp.float32), 0.1, 1.9)
    encode_weights = scatter_about(keys[13], (7, L, L), L ** -0.5, 0.25)
    encode_gains = jnp.clip(1.0 + 0.18 * jax.random.normal(keys[14], (2, L), jnp.float32), 0.1, 1.9)
    mesh_weights = scatter_about(keys[15], (LAYERS, 7, L, L), L ** -0.5, 0.25)
    mesh_gains = jnp.clip(1.0 + 0.18 * jax.random.normal(keys[16], (LAYERS, 2, L), jnp.float32), 0.1, 1.9)
    decode_weights = scatter_about(keys[17], (7, L, L), L ** -0.5, 0.25)
    decode_gains = jnp.clip(1.0 + 0.18 * jax.random.normal(keys[18], (2, L), jnp.float32), 0.1, 1.9)
    return {"grid_features": grid_features, "mesh_latent": mesh_latent, "encode_edges": encode_edges, "encode_senders": encode_senders, "encode_targets": encode_targets, "mesh_edges": mesh_edges, "mesh_senders": mesh_senders, "mesh_targets": mesh_targets, "decode_edges": decode_edges, "decode_senders": decode_senders, "embed_first": embed_first, "embed_second": embed_second, "embed_gain": embed_gain, "encode_weights": encode_weights, "encode_gains": encode_gains, "mesh_weights": mesh_weights, "mesh_gains": mesh_gains, "decode_weights": decode_weights, "decode_gains": decode_gains}


epsilon = 1e-05

def product(matrix, factor):
    return jnp.dot(matrix, factor, preferred_element_type=jnp.float32)

def project_all(stacked, factor):
    flat = stacked.reshape(-1, stacked.shape[-1])
    return product(flat, factor).reshape(stacked.shape[:-1] + (factor.shape[1],))

def normed(values, scales):
    average = lax.optimization_barrier(jnp.mean(values, axis=-1, keepdims=True))
    centred = values - average
    variance = lax.optimization_barrier(jnp.mean(centred * centred, axis=-1, keepdims=True))
    return centred * lax.rsqrt(variance + epsilon) * scales.astype(jnp.float32)

def perceptron(before, second, scales):
    hidden = jax.nn.silu(before).astype(jnp.bfloat16)
    return normed(product(hidden, second), scales)

def node_update(own_rows, summed, weights, scales):
    before = product(own_rows, weights[4]) + product(summed.astype(jnp.bfloat16), weights[5])
    return (own_rows.astype(jnp.float32) + perceptron(before, weights[6], scales)).astype(jnp.bfloat16)

def bordered(stacked):
    return jnp.pad(stacked, ((1, 1), (1, 1), (0, 0), (0, 0)))

def surround(padded, band_index, sector_index):
    zero_index = jnp.zeros((), jnp.int32)
    blocks = lax.dynamic_slice(padded, (band_index, sector_index, zero_index, zero_index), (3, 3, padded.shape[2], padded.shape[3]))
    return blocks.reshape(9 * padded.shape[2], padded.shape[3])

def reference(grid_features, mesh_latent, encode_edges, encode_senders, encode_targets, mesh_edges, mesh_senders, mesh_targets, decode_edges, decode_senders, embed_first, embed_second, embed_gain, encode_weights, encode_gains, mesh_weights, mesh_gains, decode_weights, decode_gains):
    device_ids = jnp.arange(N_GRID * N_DOM, dtype=jnp.int32)
    flat_features = grid_features.reshape(-1, C_IN)
    grid_latent = perceptron(product(flat_features, embed_first), embed_second, embed_gain)
    grid_latent = grid_latent.astype(jnp.bfloat16).reshape(N_GRID, N_DOM, G_DEV, L)
    grid_padded = bordered(project_all(grid_latent, encode_weights[1]).astype(jnp.bfloat16))

    def encode_device(device_index):
        band_index = device_index // N_DOM
        sector_index = device_index % N_DOM
        lookup = surround(grid_padded, band_index, sector_index)
        own_rows = mesh_latent[band_index, sector_index]
        targets = encode_targets[band_index, sector_index]
        receiver = product(own_rows, encode_weights[2]).astype(jnp.bfloat16)
        before = product(encode_edges[band_index, sector_index], encode_weights[0])
        before = before + jnp.take(lookup, encode_senders[band_index, sector_index], axis=0).astype(jnp.float32)
        before = before + jnp.take(receiver, jnp.minimum(targets, M_DEV - 1), axis=0).astype(jnp.float32)
        message = perceptron(before, encode_weights[3], encode_gains[0])
        summed = jax.ops.segment_sum(message, targets, num_segments=M_DEV + 1)[:M_DEV]
        return node_update(own_rows, summed, encode_weights, encode_gains[1])
    mesh_state = lax.map(encode_device, device_ids).reshape(N_GRID, N_DOM, M_DEV, L)
    edge_state = mesh_edges
    for layer_index in range(LAYERS):
        weights = mesh_weights[layer_index]
        scales = mesh_gains[layer_index]
        mesh_send = project_all(mesh_state, weights[1]).astype(jnp.bfloat16)
        mesh_padded = bordered(mesh_send)
        coarse_rows = mesh_send[:, :, :COARSE_DEV].reshape(-1, L)

        def mesh_device(device_index, weights=weights, scales=scales, mesh_padded=mesh_padded, coarse_rows=coarse_rows, mesh_state=mesh_state, edge_state=edge_state):
            band_index = device_index // N_DOM
            sector_index = device_index % N_DOM
            lookup = jnp.concatenate([surround(mesh_padded, band_index, sector_index), coarse_rows], axis=0)
            own_rows = mesh_state[band_index, sector_index]
            edge_rows = edge_state[band_index, sector_index]
            targets = mesh_targets[band_index, sector_index]
            receiver = product(own_rows, weights[2]).astype(jnp.bfloat16)
            before = product(edge_rows, weights[0])
            before = before + jnp.take(lookup, mesh_senders[band_index, sector_index], axis=0).astype(jnp.float32)
            before = before + jnp.take(receiver, targets, axis=0).astype(jnp.float32)
            message = perceptron(before, weights[3], scales[0])
            edge_next = (edge_rows.astype(jnp.float32) + message).astype(jnp.bfloat16)
            summed = jax.ops.segment_sum(message, targets, num_segments=M_DEV)
            return (node_update(own_rows, summed, weights, scales[1]), edge_next)
        mesh_next, edge_next = lax.map(mesh_device, device_ids)
        mesh_state = mesh_next.reshape(N_GRID, N_DOM, M_DEV, L)
        edge_state = edge_next.reshape(N_GRID, N_DOM, MESH_EDGES_DEV, L)
    decode_padded = bordered(project_all(mesh_state, decode_weights[1]).astype(jnp.bfloat16))

    def decode_device(device_index):
        band_index = device_index // N_DOM
        sector_index = device_index % N_DOM
        lookup = surround(decode_padded, band_index, sector_index)
        own_rows = grid_latent[band_index, sector_index]
        receiver = product(own_rows, decode_weights[2]).astype(jnp.bfloat16)
        before = product(decode_edges[band_index, sector_index], decode_weights[0])
        before = before + jnp.take(lookup, decode_senders[band_index, sector_index], axis=0).astype(jnp.float32)
        before = before + jnp.repeat(receiver, 3, axis=0).astype(jnp.float32)
        message = perceptron(before, decode_weights[3], decode_gains[0])
        summed = message.reshape(G_DEV, 3, L).sum(axis=1)
        return node_update(own_rows, summed, decode_weights, decode_gains[1])
    grid_out = lax.map(decode_device, device_ids).reshape(N_GRID, N_DOM, G_DEV, L)
    return (grid_out, mesh_state)
```

```python
import jax
import jax.numpy as jnp
from jax import lax
from jax.experimental import pallas as pl
from jax.experimental.pallas import tpu as pltpu
from jax.sharding import PartitionSpec as P

L = 512
C_IN = 474
G = 512
M = 256
CO = 16
RIM_G = 64
RIM_M = 32
ENC = 1024
EDGES = 2048
DEC = 1536
LAYERS = 2
BLOCK = 256
DEC_BLOCK = 384
NODE_BLOCK = DEC_BLOCK // 3
EPS = 1e-05
MESH = pl.DeviceIdType.MESH
BF = jnp.bfloat16
F32 = jnp.float32
I32 = jnp.int32

ROW_MS, ROW_MT, ROW_DS, ROW_ES, ROW_ET = 0, 16, 32, 44, 52

ORDERS = ("yzx", "xyz", "zxy", "yxz")


def dot(a, b):
    return jnp.dot(a, b, preferred_element_type=F32)


def silu(x):
    half = 0.5 * x
    return (half + half * jnp.tanh(half)).astype(BF)


def normed(values, gain):
    centred = values - jnp.mean(values, axis=-1, keepdims=True)
    variance = jnp.mean(centred * centred, axis=-1, keepdims=True)
    return centred * lax.rsqrt(variance + EPS) * gain


def onehot(same):
    return jnp.where(same, 1.0, 0.0).astype(BF)


def kernel(
    feat_h, mlat_h, eedge_h, esnd_h, etgt_h, medge_h, msnd_h, mtgt_h, dedge_h, dsnd_h,
    ew1_h, ew2_h, eg_h, encw_h, encg_h, mw_h, mg_h, decw_h, decg_h,
    gout_h, mout_h,
    feat, mlat, eedge, esnd, etgt, medge, msnd, mtgt, dedge, dsnd,
    ew1, ew2, eg, encw, encg, mw, mg, decw, decg,
    page, wide, hot_e, hot_m, hot_d, sum_e, sum_m,
    glat, gown, grim, mown, mrim, coarse, recv, before, msgs, node, state, mout,
    in_sem, out_sem, rim_send, rim_recv, ag_send, ag_recv,
):
    band = lax.axis_index("grid")
    sector = lax.axis_index("dom")
    x, core = band // 2, band % 2
    z, y = sector // 4, sector % 4
    own = {"x": x, "y": y, "z": z}

    def place(coords, on_core):
        return (coords["x"] * 2 + on_core, coords["z"] * 4 + coords["y"])

    loads = {}

    def load(name, src, dst):
        copy = pltpu.make_async_copy(src, dst, in_sem.at[len(loads)])
        copy.start()
        loads[name] = copy

    def loaded(*names):
        for name in names:
            loads[name].wait()

    load("feat", feat_h, feat)
    load("ew1", ew1_h, ew1)
    load("ew2", ew2_h, ew2)
    load("eg", eg_h, eg)
    load("encw1", encw_h.at[pl.ds(0, 3)], encw.at[pl.ds(0, 3)])
    load("msnd", msnd_h, msnd)
    load("mtgt", mtgt_h, mtgt)
    load("dsnd", dsnd_h, dsnd)
    load("esnd", esnd_h, esnd)
    load("etgt", etgt_h, etgt)
    load("mlat", mlat_h, mlat)
    load("eedge", eedge_h, eedge)
    load("encw2", encw_h.at[pl.ds(3, 4)], encw.at[pl.ds(3, 4)])
    load("encg", encg_h, encg)
    load("mg", mg_h, mg)
    load("medge", medge_h, medge)
    load("mw0", mw_h.at[0], mw.at[0])
    load("decg", decg_h, decg)
    load("dedge", dedge_h, dedge)
    load("decw", decw_h, decw)
    load("mw1", mw_h.at[1], mw.at[1])

    def offset_of(r):
        return r // 3 - 1, r % 3 - 1

    def inside(i, j):
        row, column = band + i, sector + j
        return (row >= 0) & (row < 8) & (column >= 0) & (column < 16)

    def slot_of(r):
        return r if r < 4 else r - 1

    around = [r for r in range(9) if r != 4]

    barrier = pltpu.get_barrier_semaphore()
    met = jnp.int32(10)
    for r in around:
        i, j = offset_of(r)
        met = met + inside(i, j).astype(I32)

        @pl.when(inside(i, j))
        def _():
            pl.semaphore_signal(barrier, inc=1, device_id=(band + i, sector + j), device_id_type=MESH)

    for axis in "xyz":
        for k in range(1, 4):
            peer = place({**own, axis: (own[axis] + k) % 4}, core)
            pl.semaphore_signal(barrier, inc=1, device_id=peer, device_id_type=MESH)
    partner = place(own, 1 - core)
    pl.semaphore_signal(barrier, inc=1, device_id=partner, device_id_type=MESH)

    def rim_copy(rows, rim, width, turn, r_to):
        i, j = offset_of(r_to)
        slot = slot_of(8 - r_to)
        first = rows.shape[0] - width if r_to > 4 else 0
        return pltpu.make_async_remote_copy(
            src_ref=rows.at[pl.ds(first, width)],
            dst_ref=rim.at[pl.ds(slot * width, width)],
            send_sem=rim_send.at[turn, slot],
            recv_sem=rim_recv.at[turn, slot],
            device_id=(band + i, sector + j),
            device_id_type=MESH,
        )

    def rim_start(rows, rim, width, turn):
        for r_to in around:
            @pl.when(inside(*offset_of(r_to)))
            def _():
                rim_copy(rows, rim, width, turn, r_to).start()

            r_from = 8 - r_to
            slot = slot_of(r_from)

            @pl.when(jnp.logical_not(inside(*offset_of(r_from))))
            def _():
                rim[pl.ds(slot * width, width), :] = jnp.zeros((width, L), BF)

    def rim_wait(rows, rim, width, turn):
        for r_from in around:
            @pl.when(inside(*offset_of(r_from)))
            def _():
                rim_copy(rows, rim, width, turn, 8 - r_from).wait_recv()

    def rim_sent(rows, rim, width, turn):
        for r_to in around:
            @pl.when(inside(*offset_of(r_to)))
            def _():
                rim_copy(rows, rim, width, turn, r_to).wait_send()

    ALL = slice(None)

    def coarse_piece(turn, c, done, coords, on_core):
        at = {a: (ALL if a in done else coords[a]) for a in "xyz"}
        return coarse.at[turn, c, at["x"], on_core, at["z"], at["y"]]

    def ag_copy(turn, c, phase, k):
        order = ORDERS[c]
        sem = (c * 4 + phase) * 4 + k
        if phase < 3:
            axis = order[phase]
            piece = coarse_piece(turn, c, order[:phase], own, core)
            peer = place({**own, axis: (own[axis] + k) % 4}, core)
        else:
            axis = order[2]
            piece = coarse_piece(turn, c, order[:2], {**own, axis: (own[axis] + 4 - k) % 4}, core)
            peer = partner
        return pltpu.make_async_remote_copy(
            src_ref=piece,
            dst_ref=piece,
            send_sem=ag_send.at[turn, sem],
            recv_sem=ag_recv.at[turn, sem],
            device_id=peer,
            device_id_type=MESH,
        )

    def ag_arrived(turn, c, phase, k):
        order = ORDERS[c]
        sem = (c * 4 + phase) * 4 + k
        axis = order[min(phase, 2)]
        done = order[: min(phase, 2)]
        coords = {**own, axis: (own[axis] + 4 - k) % 4}
        piece = coarse_piece(turn, c, done, coords, core if phase < 3 else 1 - core)
        pltpu.make_async_remote_copy(
            src_ref=piece,
            dst_ref=piece,
            send_sem=ag_send.at[turn, sem],
            recv_sem=ag_recv.at[turn, sem],
            device_id=partner,
            device_id_type=MESH,
        ).wait_recv()

    def ag_step(turn, phase):
        chunks = range(4)
        if phase == 0:
            for c in chunks:
                for k in (2, 1, 3):
                    ag_copy(turn, c, 0, k).start()
        elif phase < 3:
            for c in chunks:
                for k in (1, 3, 2):
                    ag_arrived(turn, c, phase - 1, k)
                for k in (2, 1, 3):
                    ag_copy(turn, c, phase, k).start()
                if phase == 2:
                    ag_copy(turn, c, 3, 0).start()
        elif phase == 3:
            for k in (1, 3, 2):
                for c in chunks:
                    ag_arrived(turn, c, 2, k)
                    ag_copy(turn, c, 3, k).start()
        else:
            for k in (0, 1, 3, 2):
                for c in chunks:
                    ag_arrived(turn, c, 3, k)

    def ag_sent(turn):
        for c in range(4):
            for phase in range(4):
                for k in range(0 if phase == 3 else 1, 4):
                    ag_copy(turn, c, phase, k).wait_send()

    loaded("feat", "ew1")
    hidden = silu(
        lax.dot_general(feat[...], ew1[...], (((0,), (0,)), ((), ())), preferred_element_type=F32)
    )
    loaded("ew2", "eg")
    glat[...] = normed(dot(hidden, ew2[...]), eg[...]).astype(BF)
    loaded("encw1")
    gown[...] = dot(glat[...], encw[1]).astype(BF)
    pl.semaphore_wait(barrier, met)
    rim_start(gown, grim, RIM_G, 0)

    loaded("msnd", "mtgt", "dsnd", "esnd", "etgt")
    page[...] = jnp.zeros_like(page)
    for ref, row in ((msnd, ROW_MS), (mtgt, ROW_MT), (dsnd, ROW_DS), (esnd, ROW_ES), (etgt, ROW_ET)):
        for n in range(ref.shape[1] // 128):
            page[row + n : row + n + 1, :] = ref[:, n * 128 : (n + 1) * 128]
    turned = page[...].T

    def spread(row, count):
        for n in range(count):
            wide[n * 128 : (n + 1) * 128, :] = jnp.broadcast_to(
                turned[:, row + n : row + n + 1], (128, 128)
            )

    def lanes(rows):
        return lax.broadcasted_iota(I32, (rows, 128), 1)

    def hot_columns(out, first, base, count, step):
        def body(n, _):
            rows = pl.ds(pl.multiple_of(n * step, step), step)
            values = wide[rows, :]
            ids = lanes(step)
            for t, start in enumerate(base):
                column = first + t * 128
                out[rows, column : column + 128] = onehot(values == ids + start)
            return 0

        lax.fori_loop(0, count // step, body, 0)

    def near_base(total, width):
        return [4 * total + n * 128 for n in range(total // 128)]

    def hot_rim(out, first, total, width, count, step):
        def body(n, _):
            rows = pl.ds(pl.multiple_of(n * step, step), step)
            values = wide[rows, :]
            per = 128 // width
            for t in range(8 * width // 128):
                lane = lanes(step)
                slot = t * per + lane // width
                r = jnp.where(slot < 4, slot, slot + 1)
                ids = r * total + jnp.where(slot < 4, total - width, 0) + lane % width
                column = first + t * 128
                out[rows, column : column + 128] = onehot(values == ids)
            return 0

        lax.fori_loop(0, count // step, body, 0)

    def hot_targets(out, row, count):
        for n in range(count // 128):
            ids = lax.broadcasted_iota(I32, (M, 128), 0)
            out[:, n * 128 : (n + 1) * 128] = onehot(ids == page[row + n : row + n + 1, :])

    spread(ROW_ET, ENC // 128)
    hot_columns(hot_e, 0, [0, 128], ENC, 128)
    spread(ROW_ES, ENC // 128)
    hot_columns(hot_e, M, near_base(G, RIM_G), ENC, 128)
    hot_rim(hot_e, M + G, G, RIM_G, ENC, 128)
    hot_targets(sum_e, ROW_ET, ENC)
    spread(ROW_MT, EDGES // 128)
    hot_columns(hot_m, 0, [0, 128], EDGES, 128)
    spread(ROW_MS, EDGES // 128)
    hot_columns(hot_m, M, near_base(M, RIM_M), EDGES, 128)
    hot_rim(hot_m, 2 * M, M, RIM_M, EDGES, 128)
    hot_columns(hot_m, 3 * M, [9 * M + n * 128 for n in range(16)], EDGES, 128)
    hot_targets(sum_m, ROW_MT, EDGES)
    spread(ROW_DS, DEC // 128)
    hot_columns(hot_d, 0, near_base(M, RIM_M), DEC, 128)
    hot_rim(hot_d, M, M, RIM_M, DEC, 128)

    loaded("mlat", "eedge")
    recv[...] = dot(mlat[...], encw[2]).astype(BF)
    loaded("encw2", "encg")
    rim_wait(gown, grim, RIM_G, 0)

    def encode_block(n, _):
        rows = pl.ds(pl.multiple_of(n * BLOCK, BLOCK), BLOCK)
        left = jnp.concatenate([eedge[rows, :], hot_e[rows, :]], axis=1)
        right = jnp.concatenate([encw[0], recv[...], gown[...], grim[...]], axis=0)
        hidden = silu(dot(left, right))
        msgs[rows, :] = normed(dot(hidden, encw[3]), encg[0:1, :]).astype(BF)
        return 0

    lax.fori_loop(0, ENC // BLOCK, encode_block, 0)

    def node_update(rows_state, own_part, summed, weight_sum, weight_out, gain):
        inner = own_part + dot(summed.astype(BF), weight_sum)
        return (rows_state.astype(F32) + normed(dot(silu(inner), weight_out), gain)).astype(BF)

    summed = dot(sum_e[...], msgs[0:ENC, :])
    state[...] = node_update(mlat[...], dot(mlat[...], encw[4]), summed, encw[5], encw[6], encg[1:2, :])

    loaded("mg", "medge")
    for layer in range(LAYERS):
        turn = layer + 1
        loaded("mw0" if layer == 0 else "mw1")
        weights = [mw.at[layer, k] for k in range(7)]
        now = state[...]
        send = dot(now, weights[1][...]).astype(BF)
        mown[layer] = send
        for c in range(4):
            coarse[layer, c, x, core, z, y] = send[0:CO, c * 128 : (c + 1) * 128]
        ag_step(layer, 0)
        rim_start(mown.at[layer], mrim.at[layer], RIM_M, turn)
        recv[...] = dot(now, weights[2][...]).astype(BF)
        node[0:M, :] = dot(now, weights[4][...])

        def first_part(n, _):
            rows = pl.ds(pl.multiple_of(n * BLOCK, BLOCK), BLOCK)
            left = jnp.concatenate([medge[rows, :], hot_m[rows, 0 : 2 * M]], axis=1)
            right = jnp.concatenate([weights[0][...], recv[...], mown[layer]], axis=0)
            before[rows, :] = dot(left, right)
            return 0

        ag_step(layer, 1)
        lax.fori_loop(0, 3, first_part, 0)
        ag_step(layer, 2)
        lax.fori_loop(3, 8, first_part, 0)
        ag_step(layer, 3)
        rim_wait(mown.at[layer], mrim.at[layer], RIM_M, turn)
        ag_step(layer, 4)

        def second_part(n, _):
            rows = pl.ds(pl.multiple_of(n * BLOCK, BLOCK), BLOCK)
            table = jnp.concatenate([coarse[layer, c].reshape(EDGES, 128) for c in range(4)], axis=1)
            right = jnp.concatenate([mrim[layer], table], axis=0)
            hidden = silu(before[rows, :] + dot(hot_m[rows, 2 * M :], right))
            message = normed(dot(hidden, weights[3][...]), mg[layer, 0:1, :])
            if layer + 1 < LAYERS:
                medge[rows, :] = (medge[rows, :].astype(F32) + message).astype(BF)
            msgs[rows, :] = message.astype(BF)
            return 0

        lax.fori_loop(0, EDGES // BLOCK, second_part, 0)
        summed = dot(sum_m[...], msgs[...])
        state[...] = node_update(now, node[0:M, :], summed, weights[5][...], weights[6][...], mg[layer, 1:2, :])

    mesh_out = pltpu.make_async_copy(state, mout_h, out_sem.at[0])
    mesh_out.start()
    loaded("decw", "decg", "dedge")
    mown[2] = dot(state[...], decw[1]).astype(BF)
    rim_start(mown.at[2], mrim.at[2], RIM_M, 3)
    node[...] = dot(glat[...], decw[4])
    rim_sent(gown, grim, RIM_G, 0)
    gown[...] = dot(glat[...], decw[2]).astype(BF)

    edge = lax.broadcasted_iota(I32, (DEC_BLOCK, NODE_BLOCK), 0) - 3 * lax.broadcasted_iota(
        I32, (DEC_BLOCK, NODE_BLOCK), 1
    )
    repeat = onehot((edge >= 0) & (edge < 3))
    edge = lax.broadcasted_iota(I32, (NODE_BLOCK, DEC_BLOCK), 1) - 3 * lax.broadcasted_iota(
        I32, (NODE_BLOCK, DEC_BLOCK), 0
    )
    gather = onehot((edge >= 0) & (edge < 3))

    def decode_first(n, _):
        rows = pl.ds(pl.multiple_of(n * DEC_BLOCK, DEC_BLOCK), DEC_BLOCK)
        nodes = pl.ds(pl.multiple_of(n * NODE_BLOCK, NODE_BLOCK), NODE_BLOCK)
        left = jnp.concatenate([dedge[rows, :], hot_d[rows, 0:M], repeat], axis=1)
        right = jnp.concatenate([decw[0], mown[2], gown[nodes, :]], axis=0)
        before[rows, :] = dot(left, right)
        return 0

    lax.fori_loop(0, DEC // DEC_BLOCK, decode_first, 0)
    rim_wait(mown.at[2], mrim.at[2], RIM_M, 3)

    def decode_second(n, _):
        rows = pl.ds(pl.multiple_of(n * DEC_BLOCK, DEC_BLOCK), DEC_BLOCK)
        nodes = pl.ds(pl.multiple_of(n * NODE_BLOCK, NODE_BLOCK), NODE_BLOCK)
        hidden = silu(before[rows, :] + dot(hot_d[rows, M:], mrim[2]))
        message = normed(dot(hidden, decw[3]), decg[0:1, :]).astype(BF)
        summed = dot(gather, message)
        mout[nodes, :] = node_update(
            glat[nodes, :], node[nodes, :], summed, decw[5], decw[6], decg[1:2, :]
        )
        return 0

    lax.fori_loop(0, DEC // DEC_BLOCK, decode_second, 0)
    grid_out = pltpu.make_async_copy(mout, gout_h, out_sem.at[1])
    grid_out.start()

    for layer in range(LAYERS):
        ag_sent(layer)
        rim_sent(mown.at[layer], mrim.at[layer], RIM_M, layer + 1)
    rim_sent(mown.at[2], mrim.at[2], RIM_M, 3)
    mesh_out.wait()
    grid_out.wait()


def per_device(
    grid_features, mesh_latent, encode_edges, encode_senders, encode_targets,
    mesh_edges, mesh_senders, mesh_targets, decode_edges, decode_senders,
    embed_first, embed_second, embed_gain, encode_weights, encode_gains,
    mesh_weights, mesh_gains, decode_weights, decode_gains,
):
    operands = (
        jnp.swapaxes(grid_features[0, 0], 0, 1), mesh_latent[0, 0], encode_edges[0, 0],
        encode_senders[0], encode_targets[0], mesh_edges[0, 0], mesh_senders[0],
        mesh_targets[0], decode_edges[0, 0], decode_senders[0], embed_first, embed_second,
        embed_gain[None], encode_weights, encode_gains, mesh_weights, mesh_gains,
        decode_weights, decode_gains,
    )
    scratch = [pltpu.VMEM(a.shape, a.dtype) for a in operands] + [
        pltpu.VMEM((128, 128), I32),
        pltpu.VMEM((EDGES, 128), I32),
        pltpu.VMEM((ENC, M + 2 * G), BF),
        pltpu.VMEM((EDGES, 3 * M + EDGES), BF),
        pltpu.VMEM((DEC, 2 * M), BF),
        pltpu.VMEM((M, ENC), BF),
        pltpu.VMEM((M, EDGES), BF),
        pltpu.VMEM((G, L), BF),
        pltpu.VMEM((G, L), BF),
        pltpu.VMEM((8 * RIM_G, L), BF),
        pltpu.VMEM((3, M, L), BF),
        pltpu.VMEM((3, 8 * RIM_M, L), BF),
        pltpu.VMEM((LAYERS, 4, 4, 2, 4, 4, CO, 128), BF),
        pltpu.VMEM((M, L), BF),
        pltpu.VMEM((EDGES, L), F32),
        pltpu.VMEM((EDGES, L), BF),
        pltpu.VMEM((G, L), F32),
        pltpu.VMEM((M, L), BF),
        pltpu.VMEM((G, L), BF),
        pltpu.SemaphoreType.DMA((24,)),
        pltpu.SemaphoreType.DMA((2,)),
        pltpu.SemaphoreType.DMA((4, 8)),
        pltpu.SemaphoreType.DMA((4, 8)),
        pltpu.SemaphoreType.DMA((LAYERS, 64)),
        pltpu.SemaphoreType.DMA((LAYERS, 64)),
    ]
    grid_out, mesh_out = pl.pallas_call(
        kernel,
        out_shape=(
            jax.ShapeDtypeStruct((G, L), BF),
            jax.ShapeDtypeStruct((M, L), BF),
        ),
        in_specs=[pl.BlockSpec(memory_space=pl.ANY)] * len(operands),
        out_specs=(pl.BlockSpec(memory_space=pl.ANY), pl.BlockSpec(memory_space=pl.ANY)),
        scratch_shapes=scratch,
        compiler_params=pltpu.CompilerParams(
            collective_id=0, has_side_effects=True, vmem_limit_bytes=62 * 1024 * 1024
        ),
        cost_estimate=pl.CostEstimate(
            flops=60_000_000_000, bytes_accessed=21_000_000, transcendentals=4_000_000
        ),
    )(*operands)
    return (grid_out[None, None], mesh_out[None, None])


def solution(mesh):
    block, row = P("grid", "dom", None, None), P("grid", "dom", None)
    return jax.shard_map(
        per_device,
        mesh=mesh,
        in_specs=(block, block, block, row, row, block, row, row, block, row) + (P(),) * 9,
        out_specs=(block, block),
        check_vma=False,
    )
```

```python
import jax
import jax.numpy as jnp
from jax import lax
from jax.experimental import pallas as pl
from jax.experimental.pallas import tpu as pltpu
from jax.sharding import PartitionSpec as P

L = 512
C_IN = 474
G = 512
M = 256
CO = 16
RIM_G = 64
RIM_M = 32
ENC = 1024
EDGES = 2048
DEC = 1536
LAYERS = 2
BLOCK = 256
DEC_BLOCK = 384
NODE_BLOCK = DEC_BLOCK // 3
EPS = 1e-05
MESH = pl.DeviceIdType.MESH
BF = jnp.bfloat16
F32 = jnp.float32
I32 = jnp.int32

ROW_MS, ROW_MT, ROW_DS, ROW_ES, ROW_ET = 0, 16, 32, 44, 52


def dot(a, b):
    return jnp.dot(a, b, preferred_element_type=F32)


def silu(x):
    half = 0.5 * x
    return (half + half * jnp.tanh(half)).astype(BF)


def normed(values, gain):
    centred = values - jnp.mean(values, axis=-1, keepdims=True)
    variance = jnp.mean(centred * centred, axis=-1, keepdims=True)
    return centred * lax.rsqrt(variance + EPS) * gain


def onehot(same):
    return jnp.where(same, 1.0, 0.0).astype(BF)


def kernel(
    feat_h, mlat_h, eedge_h, esnd_h, etgt_h, medge_h, msnd_h, mtgt_h, dedge_h, dsnd_h,
    ew1_h, ew2_h, eg_h, encw_h, encg_h, mw_h, mg_h, decw_h, decg_h,
    gout_h, mout_h,
    feat, mlat, eedge, esnd, etgt, medge, msnd, mtgt, dedge, dsnd,
    ew1, ew2, eg, encw, encg, mw, mg, decw, decg,
    page, wide, hot_e, hot_m, hot_d, sum_e, sum_m,
    glat, gown, grim, mown, mrim, coarse, recv, before, msgs, node, state, mout,
    in_sem, out_sem, rim_send, rim_recv, ag_send, ag_recv,
):
    band = lax.axis_index("grid")
    sector = lax.axis_index("dom")
    x, core = band // 2, band % 2
    z, y = sector // 4, sector % 4

    loads = {}

    def load(name, src, dst):
        copy = pltpu.make_async_copy(src, dst, in_sem.at[len(loads)])
        copy.start()
        loads[name] = copy

    def loaded(*names):
        for name in names:
            loads[name].wait()

    load("feat", feat_h, feat)
    load("ew1", ew1_h, ew1)
    load("ew2", ew2_h, ew2)
    load("eg", eg_h, eg)
    load("encw1", encw_h.at[pl.ds(0, 3)], encw.at[pl.ds(0, 3)])
    load("msnd", msnd_h, msnd)
    load("mtgt", mtgt_h, mtgt)
    load("dsnd", dsnd_h, dsnd)
    load("esnd", esnd_h, esnd)
    load("etgt", etgt_h, etgt)
    load("mlat", mlat_h, mlat)
    load("eedge", eedge_h, eedge)
    load("encw2", encw_h.at[pl.ds(3, 4)], encw.at[pl.ds(3, 4)])
    load("encg", encg_h, encg)
    load("mg", mg_h, mg)
    load("medge", medge_h, medge)
    load("mw0", mw_h.at[0], mw.at[0])
    load("decg", decg_h, decg)
    load("dedge", dedge_h, dedge)
    load("decw", decw_h, decw)
    load("mw1", mw_h.at[1], mw.at[1])

    def offset_of(r):
        return r // 3 - 1, r % 3 - 1

    def inside(i, j):
        row, column = band + i, sector + j
        return (row >= 0) & (row < 8) & (column >= 0) & (column < 16)

    def slot_of(r):
        return r if r < 4 else r - 1

    around = [r for r in range(9) if r != 4]

    def pick(on_zero, on_one):
        return on_zero * (1 - core) + on_one * core

    g, t = pick(z, x), pick(x, z)

    def back(value):
        return lax.rem(value + 4, 4)

    def at_core(gv, tv, yv):
        return (pick(tv, gv) * 2 + core, pick(gv, tv) * 4 + yv)

    plane = [(dg, dy) for dg in (2, 1, 3, 0) for dy in (2, 1, 3, 0) if dg + dy]
    partner = (x * 2 + 1 - core, sector)

    barrier = pltpu.get_barrier_semaphore()
    met = jnp.int32(19)
    for r in around:
        i, j = offset_of(r)
        met = met + inside(i, j).astype(I32)

        @pl.when(inside(i, j))
        def _():
            pl.semaphore_signal(barrier, inc=1, device_id=(band + i, sector + j), device_id_type=MESH)

    for dg, dy in plane:
        peer = at_core(back(g + dg), t, back(y + dy))
        pl.semaphore_signal(barrier, inc=1, device_id=peer, device_id_type=MESH)
    for k in range(1, 4):
        pl.semaphore_signal(barrier, inc=1, device_id=at_core(g, back(t + k), y), device_id_type=MESH)
    pl.semaphore_signal(barrier, inc=1, device_id=partner, device_id_type=MESH)

    def rim_copy(rows, rim, width, turn, r_to):
        i, j = offset_of(r_to)
        slot = slot_of(8 - r_to)
        first = rows.shape[0] - width if r_to > 4 else 0
        return pltpu.make_async_remote_copy(
            src_ref=rows.at[pl.ds(first, width)],
            dst_ref=rim.at[pl.ds(slot * width, width)],
            send_sem=rim_send.at[turn, slot],
            recv_sem=rim_recv.at[turn, slot],
            device_id=(band + i, sector + j),
            device_id_type=MESH,
        )

    def rim_start(rows, rim, width, turn):
        for r_to in around:
            @pl.when(inside(*offset_of(r_to)))
            def _():
                rim_copy(rows, rim, width, turn, r_to).start()

            r_from = 8 - r_to
            slot = slot_of(r_from)

            @pl.when(jnp.logical_not(inside(*offset_of(r_from))))
            def _():
                rim[pl.ds(slot * width, width), :] = jnp.zeros((width, L), BF)

    def rim_wait(rows, rim, width, turn):
        for r_from in around:
            @pl.when(inside(*offset_of(r_from)))
            def _():
                rim_copy(rows, rim, width, turn, 8 - r_from).wait_recv()

    def rim_sent(rows, rim, width, turn):
        for r_to in around:
            @pl.when(inside(*offset_of(r_to)))
            def _():
                rim_copy(rows, rim, width, turn, r_to).wait_send()

    def ag_copy(turn, piece, sem, peer):
        return pltpu.make_async_remote_copy(
            src_ref=piece,
            dst_ref=piece,
            send_sem=ag_send.at[turn, sem],
            recv_sem=ag_recv.at[turn, sem],
            device_id=peer,
            device_id_type=MESH,
        )

    def group(turn, gv, tv):
        return coarse.at[turn, pick(tv, gv), core, pick(gv, tv)]

    def plane_send(turn, dg, dy):
        piece = coarse.at[turn, x, core, z, y]
        return ag_copy(turn, piece, dg * 4 + dy, at_core(back(g + dg), t, back(y + dy)))

    def plane_come(turn, dg, dy):
        gv = back(g - dg)
        piece = coarse.at[turn, pick(t, gv), core, pick(gv, t), back(y - dy)]
        return ag_copy(turn, piece, dg * 4 + dy, partner)

    def line_send(turn, dg, k):
        return ag_copy(turn, group(turn, back(g - dg), t), 16 + dg * 4 + k, at_core(g, back(t + k), y))

    def line_come(turn, dg, k):
        return ag_copy(turn, group(turn, back(g - dg), back(t - k)), 16 + dg * 4 + k, partner)

    def core_send(turn, dg, k):
        return ag_copy(turn, group(turn, back(g - dg), back(t - k)), 32 + dg * 4 + k, partner)

    def core_come(turn, dg, k):
        gv, tv = back(t - dg), back(g - k)
        piece = coarse.at[turn, pick(gv, tv), 1 - core, pick(tv, gv)]
        return ag_copy(turn, piece, 32 + dg * 4 + k, partner)

    def ag_start(turn):
        for dg, dy in plane:
            plane_send(turn, dg, dy).start()

    def ag_second(turn):
        for dg in (0, 1, 3, 2):
            for dy in (0, 1, 3, 2):
                if dg + dy:
                    plane_come(turn, dg, dy).wait_recv()
            for k in (2, 1, 3):
                line_send(turn, dg, k).start()
            core_send(turn, dg, 0).start()

    def ag_third(turn):
        for dg in (0, 1, 3, 2):
            for k in (1, 3, 2):
                line_come(turn, dg, k).wait_recv()
                core_send(turn, dg, k).start()

    def ag_last(turn):
        for dg in (0, 1, 3, 2):
            for k in (0, 1, 3, 2):
                core_come(turn, dg, k).wait_recv()

    def ag_sent(turn):
        for dg, dy in plane:
            plane_send(turn, dg, dy).wait_send()
        for dg in range(4):
            for k in range(4):
                if k:
                    line_send(turn, dg, k).wait_send()
                core_send(turn, dg, k).wait_send()

    loaded("feat", "ew1")
    hidden = silu(
        lax.dot_general(feat[...], ew1[...], (((0,), (0,)), ((), ())), preferred_element_type=F32)
    )
    loaded("ew2", "eg")
    glat[...] = normed(dot(hidden, ew2[...]), eg[...]).astype(BF)
    loaded("encw1")
    gown[...] = dot(glat[...], encw[1]).astype(BF)
    pl.semaphore_wait(barrier, met)
    rim_start(gown, grim, RIM_G, 0)

    loaded("msnd", "mtgt", "dsnd", "esnd", "etgt")
    page[...] = jnp.zeros_like(page)
    for ref, row in ((msnd, ROW_MS), (mtgt, ROW_MT), (dsnd, ROW_DS), (esnd, ROW_ES), (etgt, ROW_ET)):
        for n in range(ref.shape[1] // 128):
            page[row + n : row + n + 1, :] = ref[:, n * 128 : (n + 1) * 128]
    turned = page[...].T

    def spread(row, count):
        for n in range(count):
            wide[n * 128 : (n + 1) * 128, :] = jnp.broadcast_to(
                turned[:, row + n : row + n + 1], (128, 128)
            )

    def lanes(rows):
        return lax.broadcasted_iota(I32, (rows, 128), 1)

    def hot_columns(out, first, base, count, step):
        def body(n, _):
            rows = pl.ds(pl.multiple_of(n * step, step), step)
            values = wide[rows, :]
            ids = lanes(step)
            for t, start in enumerate(base):
                column = first + t * 128
                out[rows, column : column + 128] = onehot(values == ids + start)
            return 0

        lax.fori_loop(0, count // step, body, 0)

    def near_base(total, width):
        return [4 * total + n * 128 for n in range(total // 128)]

    def hot_rim(out, first, total, width, count, step):
        def body(n, _):
            rows = pl.ds(pl.multiple_of(n * step, step), step)
            values = wide[rows, :]
            per = 128 // width
            for t in range(8 * width // 128):
                lane = lanes(step)
                slot = t * per + lane // width
                r = jnp.where(slot < 4, slot, slot + 1)
                ids = r * total + jnp.where(slot < 4, total - width, 0) + lane % width
                column = first + t * 128
                out[rows, column : column + 128] = onehot(values == ids)
            return 0

        lax.fori_loop(0, count // step, body, 0)

    def hot_targets(out, row, count):
        for n in range(count // 128):
            ids = lax.broadcasted_iota(I32, (M, 128), 0)
            out[:, n * 128 : (n + 1) * 128] = onehot(ids == page[row + n : row + n + 1, :])

    spread(ROW_ET, ENC // 128)
    hot_columns(hot_e, 0, [0, 128], ENC, 128)
    spread(ROW_ES, ENC // 128)
    hot_columns(hot_e, M, near_base(G, RIM_G), ENC, 128)
    hot_rim(hot_e, M + G, G, RIM_G, ENC, 128)
    hot_targets(sum_e, ROW_ET, ENC)
    spread(ROW_MT, EDGES // 128)
    hot_columns(hot_m, 0, [0, 128], EDGES, 128)
    spread(ROW_MS, EDGES // 128)
    hot_columns(hot_m, M, near_base(M, RIM_M), EDGES, 128)
    hot_rim(hot_m, 2 * M, M, RIM_M, EDGES, 128)
    hot_columns(hot_m, 3 * M, [9 * M + n * 128 for n in range(16)], EDGES, 128)
    hot_targets(sum_m, ROW_MT, EDGES)
    spread(ROW_DS, DEC // 128)
    hot_columns(hot_d, 0, near_base(M, RIM_M), DEC, 128)
    hot_rim(hot_d, M, M, RIM_M, DEC, 128)

    loaded("mlat", "eedge")
    recv[...] = dot(mlat[...], encw[2]).astype(BF)
    loaded("encw2", "encg")
    rim_wait(gown, grim, RIM_G, 0)

    def encode_block(n, _):
        rows = pl.ds(pl.multiple_of(n * BLOCK, BLOCK), BLOCK)
        left = jnp.concatenate([eedge[rows, :], hot_e[rows, :]], axis=1)
        right = jnp.concatenate([encw[0], recv[...], gown[...], grim[...]], axis=0)
        hidden = silu(dot(left, right))
        msgs[rows, :] = normed(dot(hidden, encw[3]), encg[0:1, :]).astype(BF)
        return 0

    lax.fori_loop(0, ENC // BLOCK, encode_block, 0, unroll=4)

    def node_update(rows_state, own_part, summed, weight_sum, weight_out, gain):
        inner = own_part + dot(summed.astype(BF), weight_sum)
        return (rows_state.astype(F32) + normed(dot(silu(inner), weight_out), gain)).astype(BF)

    summed = dot(sum_e[...], msgs[0:ENC, :])
    state[...] = node_update(mlat[...], dot(mlat[...], encw[4]), summed, encw[5], encw[6], encg[1:2, :])

    loaded("mg", "medge")
    for layer in range(LAYERS):
        turn = layer + 1
        loaded("mw0" if layer == 0 else "mw1")
        weights = [mw.at[layer, k] for k in range(7)]
        now = state[...]
        send = dot(now, weights[1][...]).astype(BF)
        mown[layer] = send
        coarse[layer, x, core, z, y] = send[0:CO]
        ag_start(layer)
        recv[...] = dot(now, weights[2][...]).astype(BF)
        node[0:M, :] = dot(now, weights[4][...])

        def first_part(n, _):
            rows = pl.ds(pl.multiple_of(n * BLOCK, BLOCK), BLOCK)
            left = jnp.concatenate([medge[rows, :], hot_m[rows, 0 : 2 * M]], axis=1)
            right = jnp.concatenate([weights[0][...], recv[...], mown[layer]], axis=0)
            before[rows, :] = dot(left, right)
            return 0

        lax.fori_loop(0, EDGES // BLOCK, first_part, 0, unroll=4)
        ag_second(layer)
        rim_start(mown.at[layer], mrim.at[layer], RIM_M, turn)
        ag_third(layer)
        rim_wait(mown.at[layer], mrim.at[layer], RIM_M, turn)
        ag_last(layer)

        def second_part(n, _):
            rows = pl.ds(pl.multiple_of(n * BLOCK, BLOCK), BLOCK)
            right = jnp.concatenate([mrim[layer], coarse[layer].reshape(8 * 16 * CO, L)], axis=0)
            hidden = silu(before[rows, :] + dot(hot_m[rows, 2 * M :], right))
            message = normed(dot(hidden, weights[3][...]), mg[layer, 0:1, :])
            if layer + 1 < LAYERS:
                medge[rows, :] = (medge[rows, :].astype(F32) + message).astype(BF)
            msgs[rows, :] = message.astype(BF)
            return 0

        lax.fori_loop(0, EDGES // BLOCK, second_part, 0, unroll=4)
        summed = dot(sum_m[...], msgs[...])
        state[...] = node_update(now, node[0:M, :], summed, weights[5][...], weights[6][...], mg[layer, 1:2, :])

    mesh_out = pltpu.make_async_copy(state, mout_h, out_sem.at[0])
    mesh_out.start()
    loaded("decw", "decg", "dedge")
    mown[2] = dot(state[...], decw[1]).astype(BF)
    rim_start(mown.at[2], mrim.at[2], RIM_M, 3)
    node[...] = dot(glat[...], decw[4])
    rim_sent(gown, grim, RIM_G, 0)
    gown[...] = dot(glat[...], decw[2]).astype(BF)

    edge = lax.broadcasted_iota(I32, (DEC_BLOCK, NODE_BLOCK), 0) - 3 * lax.broadcasted_iota(
        I32, (DEC_BLOCK, NODE_BLOCK), 1
    )
    repeat = onehot((edge >= 0) & (edge < 3))
    edge = lax.broadcasted_iota(I32, (NODE_BLOCK, DEC_BLOCK), 1) - 3 * lax.broadcasted_iota(
        I32, (NODE_BLOCK, DEC_BLOCK), 0
    )
    gather = onehot((edge >= 0) & (edge < 3))

    def decode_first(n, _):
        rows = pl.ds(pl.multiple_of(n * DEC_BLOCK, DEC_BLOCK), DEC_BLOCK)
        nodes = pl.ds(pl.multiple_of(n * NODE_BLOCK, NODE_BLOCK), NODE_BLOCK)
        left = jnp.concatenate([dedge[rows, :], hot_d[rows, 0:M], repeat], axis=1)
        right = jnp.concatenate([decw[0], mown[2], gown[nodes, :]], axis=0)
        before[rows, :] = dot(left, right)
        return 0

    lax.fori_loop(0, DEC // DEC_BLOCK, decode_first, 0, unroll=4)
    rim_wait(mown.at[2], mrim.at[2], RIM_M, 3)

    def decode_second(n, _):
        rows = pl.ds(pl.multiple_of(n * DEC_BLOCK, DEC_BLOCK), DEC_BLOCK)
        nodes = pl.ds(pl.multiple_of(n * NODE_BLOCK, NODE_BLOCK), NODE_BLOCK)
        hidden = silu(before[rows, :] + dot(hot_d[rows, M:], mrim[2]))
        message = normed(dot(hidden, decw[3]), decg[0:1, :]).astype(BF)
        summed = dot(gather, message)
        mout[nodes, :] = node_update(
            glat[nodes, :], node[nodes, :], summed, decw[5], decw[6], decg[1:2, :]
        )
        return 0

    lax.fori_loop(0, DEC // DEC_BLOCK, decode_second, 0, unroll=4)
    grid_out = pltpu.make_async_copy(mout, gout_h, out_sem.at[1])
    grid_out.start()

    for layer in range(LAYERS):
        ag_sent(layer)
        rim_sent(mown.at[layer], mrim.at[layer], RIM_M, layer + 1)
    rim_sent(mown.at[2], mrim.at[2], RIM_M, 3)
    mesh_out.wait()
    grid_out.wait()


def hand_on(grid_in, mesh_in, grid_out, mesh_out):
    grid_out[...] = grid_in[...]
    mesh_out[...] = mesh_in[...]


def per_device(
    grid_features, mesh_latent, encode_edges, encode_senders, encode_targets,
    mesh_edges, mesh_senders, mesh_targets, decode_edges, decode_senders,
    embed_first, embed_second, embed_gain, encode_weights, encode_gains,
    mesh_weights, mesh_gains, decode_weights, decode_gains,
):
    operands = (
        jnp.swapaxes(grid_features[0, 0], 0, 1), mesh_latent[0, 0], encode_edges[0, 0],
        encode_senders[0], encode_targets[0], mesh_edges[0, 0], mesh_senders[0],
        mesh_targets[0], decode_edges[0, 0], decode_senders[0], embed_first, embed_second,
        embed_gain[None], encode_weights, encode_gains, mesh_weights, mesh_gains,
        decode_weights, decode_gains,
    )
    scratch = [pltpu.VMEM(a.shape, a.dtype) for a in operands] + [
        pltpu.VMEM((128, 128), I32),
        pltpu.VMEM((EDGES, 128), I32),
        pltpu.VMEM((ENC, M + 2 * G), BF),
        pltpu.VMEM((EDGES, 3 * M + EDGES), BF),
        pltpu.VMEM((DEC, 2 * M), BF),
        pltpu.VMEM((M, ENC), BF),
        pltpu.VMEM((M, EDGES), BF),
        pltpu.VMEM((G, L), BF),
        pltpu.VMEM((G, L), BF),
        pltpu.VMEM((8 * RIM_G, L), BF),
        pltpu.VMEM((3, M, L), BF),
        pltpu.VMEM((3, 8 * RIM_M, L), BF),
        pltpu.VMEM((LAYERS, 4, 2, 4, 4, CO, L), BF),
        pltpu.VMEM((M, L), BF),
        pltpu.VMEM((EDGES, L), F32),
        pltpu.VMEM((EDGES, L), BF),
        pltpu.VMEM((G, L), F32),
        pltpu.VMEM((M, L), BF),
        pltpu.VMEM((G, L), BF),
        pltpu.SemaphoreType.DMA((24,)),
        pltpu.SemaphoreType.DMA((2,)),
        pltpu.SemaphoreType.DMA((4, 8)),
        pltpu.SemaphoreType.DMA((4, 8)),
        pltpu.SemaphoreType.DMA((LAYERS, 48)),
        pltpu.SemaphoreType.DMA((LAYERS, 48)),
    ]
    grid_out, mesh_out = pl.pallas_call(
        kernel,
        out_shape=(
            jax.ShapeDtypeStruct((G, L), BF),
            jax.ShapeDtypeStruct((M, L), BF),
        ),
        in_specs=[pl.BlockSpec(memory_space=pl.ANY)] * len(operands),
        out_specs=(pl.BlockSpec(memory_space=pl.ANY), pl.BlockSpec(memory_space=pl.ANY)),
        scratch_shapes=scratch,
        compiler_params=pltpu.CompilerParams(
            collective_id=0, has_side_effects=True, vmem_limit_bytes=62 * 1024 * 1024
        ),
        cost_estimate=pl.CostEstimate(
            flops=60_000_000_000, bytes_accessed=21_000_000, transcendentals=4_000_000
        ),
    )(*operands)
    grid_out, mesh_out = pl.pallas_call(
        hand_on,
        out_shape=(
            jax.ShapeDtypeStruct((G, L), BF),
            jax.ShapeDtypeStruct((M, L), BF),
        ),
        in_specs=[pl.BlockSpec(memory_space=pltpu.VMEM)] * 2,
        out_specs=(pl.BlockSpec(memory_space=pltpu.VMEM), pl.BlockSpec(memory_space=pltpu.VMEM)),
    )(grid_out, mesh_out)
    return (grid_out[None, None], mesh_out[None, None])


def solution(mesh):
    block, row = P("grid", "dom", None, None), P("grid", "dom", None)
    return jax.shard_map(
        per_device,
        mesh=mesh,
        in_specs=(block, block, block, row, row, block, row, row, block, row) + (P(),) * 9,
        out_specs=(block, block),
        check_vma=False,
    )
```

```python
import jax
import jax.numpy as jnp
from jax import lax
from jax.experimental import pallas as pl
from jax.experimental.pallas import tpu as pltpu
from jax.sharding import PartitionSpec as P

L = 512
C_IN = 474
G = 512
M = 256
CO = 16
RIM_G = 64
RIM_M = 32
ENC = 1024
EDGES = 2048
DEC = 1536
LAYERS = 2
BLOCK = 256
WIDE = 512
DEC_BLOCK = 768
NODE_BLOCK = DEC_BLOCK // 3
EPS = 1e-05
MESH = pl.DeviceIdType.MESH
BF = jnp.bfloat16
F32 = jnp.float32
I32 = jnp.int32

ROW_MS, ROW_MT, ROW_DS, ROW_ES, ROW_ET = 0, 16, 32, 44, 52


def dot(a, b):
    return jnp.dot(a, b, preferred_element_type=F32)


def silu(x):
    half = 0.5 * x
    return (half + half * jnp.tanh(half)).astype(BF)


def normed(values, gain):
    centred = values - jnp.mean(values, axis=-1, keepdims=True)
    variance = jnp.mean(centred * centred, axis=-1, keepdims=True)
    return centred * lax.rsqrt(variance + EPS) * gain


def onehot(same):
    return jnp.where(same, 1.0, 0.0).astype(BF)


def kernel(
    feat_h, mlat_h, eedge_h, esnd_h, etgt_h, medge_h, msnd_h, mtgt_h, dedge_h, dsnd_h,
    ew1_h, ew2_h, eg_h, encw_h, encg_h, mw_h, mg_h, decw_h, decg_h,
    gout_h, mout_h,
    feat, mlat, eedge, esnd, etgt, medge, msnd, mtgt, dedge, dsnd,
    ew1, ew2, eg, encw, encg, mw, mg, decw, decg,
    page, wide, hot_e, hot_m, hot_d, sum_e, sum_m,
    glat, gown, grim, mown, mrim, coarse, recv, before, msgs, node, state, mout,
    in_sem, out_sem, rim_send, rim_recv, ag_send, ag_recv,
):
    band = lax.axis_index("grid")
    sector = lax.axis_index("dom")
    x, core = band // 2, band % 2
    z, y = sector // 4, sector % 4

    loads = {}

    def load(name, src, dst):
        copy = pltpu.make_async_copy(src, dst, in_sem.at[len(loads)])
        copy.start()
        loads[name] = copy

    def loaded(*names):
        for name in names:
            loads[name].wait()

    load("feat", feat_h, feat)
    load("ew1", ew1_h, ew1)
    load("ew2", ew2_h, ew2)
    load("eg", eg_h, eg)
    load("encw1", encw_h.at[pl.ds(0, 3)], encw.at[pl.ds(0, 3)])
    load("msnd", msnd_h, msnd)
    load("mtgt", mtgt_h, mtgt)
    load("dsnd", dsnd_h, dsnd)
    load("esnd", esnd_h, esnd)
    load("etgt", etgt_h, etgt)
    load("mlat", mlat_h, mlat)
    load("eedge", eedge_h, eedge)
    load("encw2", encw_h.at[pl.ds(3, 4)], encw.at[pl.ds(3, 4)])
    load("encg", encg_h, encg)
    load("mg", mg_h, mg)
    load("medge", medge_h, medge)
    load("mw0", mw_h.at[0], mw.at[0])
    load("decg", decg_h, decg)
    load("dedge", dedge_h, dedge)
    load("decw", decw_h, decw)
    load("mw1", mw_h.at[1], mw.at[1])

    def offset_of(r):
        return r // 3 - 1, r % 3 - 1

    def inside(i, j):
        row, column = band + i, sector + j
        return (row >= 0) & (row < 8) & (column >= 0) & (column < 16)

    def slot_of(r):
        return r if r < 4 else r - 1

    around = [r for r in range(9) if r != 4]

    def pick(on_zero, on_one):
        return on_zero * (1 - core) + on_one * core

    g, t = pick(z, x), pick(x, z)

    def back(value):
        return lax.rem(value + 4, 4)

    def at_core(gv, tv, yv):
        return (pick(tv, gv) * 2 + core, pick(gv, tv) * 4 + yv)

    plane = [(dg, dy) for dg in (2, 1, 3, 0) for dy in (2, 1, 3, 0) if dg + dy]
    partner = (x * 2 + 1 - core, sector)

    barrier = pltpu.get_barrier_semaphore()
    met = jnp.int32(19)
    for r in around:
        i, j = offset_of(r)
        met = met + inside(i, j).astype(I32)

        @pl.when(inside(i, j))
        def _():
            pl.semaphore_signal(barrier, inc=1, device_id=(band + i, sector + j), device_id_type=MESH)

    for dg, dy in plane:
        peer = at_core(back(g + dg), t, back(y + dy))
        pl.semaphore_signal(barrier, inc=1, device_id=peer, device_id_type=MESH)
    for k in range(1, 4):
        pl.semaphore_signal(barrier, inc=1, device_id=at_core(g, back(t + k), y), device_id_type=MESH)
    pl.semaphore_signal(barrier, inc=1, device_id=partner, device_id_type=MESH)

    def rim_copy(rows, rim, width, turn, r_to):
        i, j = offset_of(r_to)
        slot = slot_of(8 - r_to)
        first = rows.shape[0] - width if r_to > 4 else 0
        return pltpu.make_async_remote_copy(
            src_ref=rows.at[pl.ds(first, width)],
            dst_ref=rim.at[pl.ds(slot * width, width)],
            send_sem=rim_send.at[turn, slot],
            recv_sem=rim_recv.at[turn, slot],
            device_id=(band + i, sector + j),
            device_id_type=MESH,
        )

    def rim_start(rows, rim, width, turn):
        for r_to in around:
            @pl.when(inside(*offset_of(r_to)))
            def _():
                rim_copy(rows, rim, width, turn, r_to).start()

            r_from = 8 - r_to
            slot = slot_of(r_from)

            @pl.when(jnp.logical_not(inside(*offset_of(r_from))))
            def _():
                rim[pl.ds(slot * width, width), :] = jnp.zeros((width, L), BF)

    def rim_wait(rows, rim, width, turn):
        for r_from in around:
            @pl.when(inside(*offset_of(r_from)))
            def _():
                rim_copy(rows, rim, width, turn, 8 - r_from).wait_recv()

    def rim_sent(rows, rim, width, turn):
        for r_to in around:
            @pl.when(inside(*offset_of(r_to)))
            def _():
                rim_copy(rows, rim, width, turn, r_to).wait_send()

    def ag_copy(turn, piece, sem, peer):
        return pltpu.make_async_remote_copy(
            src_ref=piece,
            dst_ref=piece,
            send_sem=ag_send.at[turn, sem],
            recv_sem=ag_recv.at[turn, sem],
            device_id=peer,
            device_id_type=MESH,
        )

    def group(turn, gv, tv):
        return coarse.at[turn, pick(tv, gv), core, pick(gv, tv)]

    def plane_send(turn, dg, dy):
        piece = coarse.at[turn, x, core, z, y]
        return ag_copy(turn, piece, dg * 4 + dy, at_core(back(g + dg), t, back(y + dy)))

    def plane_come(turn, dg, dy):
        gv = back(g - dg)
        piece = coarse.at[turn, pick(t, gv), core, pick(gv, t), back(y - dy)]
        return ag_copy(turn, piece, dg * 4 + dy, partner)

    def line_send(turn, dg, k):
        return ag_copy(turn, group(turn, back(g - dg), t), 16 + dg * 4 + k, at_core(g, back(t + k), y))

    def line_come(turn, dg, k):
        return ag_copy(turn, group(turn, back(g - dg), back(t - k)), 16 + dg * 4 + k, partner)

    def core_send(turn, dg, k):
        return ag_copy(turn, group(turn, back(g - dg), back(t - k)), 32 + dg * 4 + k, partner)

    def core_come(turn, dg, k):
        gv, tv = back(t - dg), back(g - k)
        piece = coarse.at[turn, pick(gv, tv), 1 - core, pick(tv, gv)]
        return ag_copy(turn, piece, 32 + dg * 4 + k, partner)

    def ag_start(turn):
        for dg, dy in plane:
            plane_send(turn, dg, dy).start()

    def ag_second(turn):
        for dg in (0, 1, 3, 2):
            for dy in (0, 1, 3, 2):
                if dg + dy:
                    plane_come(turn, dg, dy).wait_recv()
            for k in (2, 1, 3):
                line_send(turn, dg, k).start()
            core_send(turn, dg, 0).start()

    def ag_third(turn):
        for dg in (0, 1, 3, 2):
            for k in (1, 3, 2):
                line_come(turn, dg, k).wait_recv()
                core_send(turn, dg, k).start()

    def ag_last(turn):
        for dg in (0, 1, 3, 2):
            for k in (0, 1, 3, 2):
                core_come(turn, dg, k).wait_recv()

    def ag_sent(turn):
        for dg, dy in plane:
            plane_send(turn, dg, dy).wait_send()
        for dg in range(4):
            for k in range(4):
                if k:
                    line_send(turn, dg, k).wait_send()
                core_send(turn, dg, k).wait_send()

    loaded("feat", "ew1")
    hidden = silu(
        lax.dot_general(feat[...], ew1[...], (((0,), (0,)), ((), ())), preferred_element_type=F32)
    )
    loaded("ew2", "eg")
    glat[...] = normed(dot(hidden, ew2[...]), eg[...]).astype(BF)
    loaded("encw1")
    gown[...] = dot(glat[...], encw[1]).astype(BF)
    pl.semaphore_wait(barrier, met)
    rim_start(gown, grim, RIM_G, 0)

    loaded("msnd", "mtgt", "dsnd", "esnd", "etgt")
    page[...] = jnp.zeros_like(page)
    for ref, row in ((msnd, ROW_MS), (mtgt, ROW_MT), (dsnd, ROW_DS), (esnd, ROW_ES), (etgt, ROW_ET)):
        for n in range(ref.shape[1] // 128):
            page[row + n : row + n + 1, :] = ref[:, n * 128 : (n + 1) * 128]
    turned = page[...].T

    def spread(row, count):
        for n in range(count):
            wide[n * 128 : (n + 1) * 128, :] = jnp.broadcast_to(
                turned[:, row + n : row + n + 1], (128, 128)
            )

    def lanes(rows):
        return lax.broadcasted_iota(I32, (rows, 128), 1)

    def hot_columns(out, first, base, count, step):
        def body(n, _):
            rows = pl.ds(pl.multiple_of(n * step, step), step)
            values = wide[rows, :]
            ids = lanes(step)
            for t, start in enumerate(base):
                column = first + t * 128
                out[rows, column : column + 128] = onehot(values == ids + start)
            return 0

        lax.fori_loop(0, count // step, body, 0)

    def near_base(total, width):
        return [4 * total + n * 128 for n in range(total // 128)]

    def hot_rim(out, first, total, width, count, step):
        def body(n, _):
            rows = pl.ds(pl.multiple_of(n * step, step), step)
            values = wide[rows, :]
            per = 128 // width
            for t in range(8 * width // 128):
                lane = lanes(step)
                slot = t * per + lane // width
                r = jnp.where(slot < 4, slot, slot + 1)
                ids = r * total + jnp.where(slot < 4, total - width, 0) + lane % width
                column = first + t * 128
                out[rows, column : column + 128] = onehot(values == ids)
            return 0

        lax.fori_loop(0, count // step, body, 0)

    def hot_targets(out, row, count):
        for n in range(count // 128):
            ids = lax.broadcasted_iota(I32, (M, 128), 0)
            out[:, n * 128 : (n + 1) * 128] = onehot(ids == page[row + n : row + n + 1, :])

    spread(ROW_ET, ENC // 128)
    hot_columns(hot_e, 0, [0, 128], ENC, 128)
    spread(ROW_ES, ENC // 128)
    hot_columns(hot_e, M, near_base(G, RIM_G), ENC, 128)
    hot_rim(hot_e, M + G, G, RIM_G, ENC, 128)
    hot_targets(sum_e, ROW_ET, ENC)
    spread(ROW_MT, EDGES // 128)
    hot_columns(hot_m, 0, [0, 128], EDGES, 128)
    spread(ROW_MS, EDGES // 128)
    hot_columns(hot_m, M, near_base(M, RIM_M), EDGES, 128)
    hot_rim(hot_m, 2 * M, M, RIM_M, EDGES, 128)
    hot_columns(hot_m, 3 * M, [9 * M + n * 128 for n in range(16)], EDGES, 128)
    hot_targets(sum_m, ROW_MT, EDGES)
    spread(ROW_DS, DEC // 128)
    hot_columns(hot_d, 0, near_base(M, RIM_M), DEC, 128)
    hot_rim(hot_d, M, M, RIM_M, DEC, 128)

    def block_rows(n):
        return pl.ds(pl.multiple_of(n * BLOCK, BLOCK), BLOCK)

    loaded("mlat", "eedge", "encw2", "encg")
    recv[...] = dot(mlat[...], encw[2]).astype(BF)
    node[0:M, :] = dot(mlat[...], encw[4])

    def encode_first(n, _):
        rows = pl.ds(pl.multiple_of(n * WIDE, WIDE), WIDE)
        left = jnp.concatenate([eedge[rows, :], hot_e[rows, 0 : M + G]], axis=1)
        right = jnp.concatenate([encw[0], recv[...], gown[...]], axis=0)
        before[rows, :] = dot(left, right)
        return 0

    lax.fori_loop(0, ENC // WIDE, encode_first, 0, unroll=2)
    rim_wait(gown, grim, RIM_G, 0)

    def encode_second(n, _):
        rows = pl.ds(pl.multiple_of(n * WIDE, WIDE), WIDE)
        hidden = silu(before[rows, :] + dot(hot_e[rows, M + G :], grim[...]))
        msgs[rows, :] = normed(dot(hidden, encw[3]), encg[0:1, :]).astype(BF)
        return 0

    lax.fori_loop(0, ENC // WIDE, encode_second, 0, unroll=2)

    def node_update(rows_state, own_part, summed, weight_sum, weight_out, gain):
        inner = own_part + dot(summed.astype(BF), weight_sum)
        return (rows_state.astype(F32) + normed(dot(silu(inner), weight_out), gain)).astype(BF)

    def mesh_update(old, count, sums, messages, weights, gain, turn):
        def update(rows):
            summed = dot(sums[0:rows, :], messages)
            return node_update(
                old[0:rows, :], node[0:rows, :], summed, weights[5], weights[6], gain
            )

        if turn < LAYERS:
            loaded("mw0" if turn == 0 else "mw1")
            coarse[turn, x, core, z, y] = dot(update(CO), mw[turn, 1]).astype(BF)
            ag_start(turn)
        state[...] = update(count)

    mesh_update(mlat, M, sum_e, msgs[0:ENC, :], encw, encg[1:2, :], 0)

    loaded("mg", "medge")
    for layer in range(LAYERS):
        turn = layer + 1
        weights = [mw.at[layer, k] for k in range(7)]
        now = state[...]
        send = dot(now, weights[1][...]).astype(BF)
        mown[layer] = send
        recv[...] = dot(now, weights[2][...]).astype(BF)
        node[0:M, :] = dot(now, weights[4][...])

        def first_part(n, _):
            rows = pl.ds(pl.multiple_of(n * BLOCK, BLOCK), BLOCK)
            left = jnp.concatenate([medge[rows, :], hot_m[rows, 0 : 2 * M]], axis=1)
            right = jnp.concatenate([weights[0][...], recv[...], mown[layer]], axis=0)
            before[rows, :] = dot(left, right)
            return 0

        ag_second(layer)
        rim_start(mown.at[layer], mrim.at[layer], RIM_M, turn)
        lax.fori_loop(0, EDGES // BLOCK, first_part, 0, unroll=4)
        if layer == 0:
            rim_sent(gown, grim, RIM_G, 0)
        else:
            ag_sent(layer - 1)
            rim_sent(mown.at[layer - 1], mrim.at[layer - 1], RIM_M, layer)
        ag_third(layer)
        rim_wait(mown.at[layer], mrim.at[layer], RIM_M, turn)
        ag_last(layer)

        def second_part(n, _):
            rows = pl.ds(pl.multiple_of(n * WIDE, WIDE), WIDE)
            right = jnp.concatenate([mrim[layer], coarse[layer].reshape(8 * 16 * CO, L)], axis=0)
            hidden = silu(before[rows, :] + dot(hot_m[rows, 2 * M :], right))
            message = normed(dot(hidden, weights[3][...]), mg[layer, 0:1, :])
            if layer + 1 < LAYERS:
                medge[rows, :] = (medge[rows, :].astype(F32) + message).astype(BF)
            msgs[rows, :] = message.astype(BF)
            return 0

        lax.fori_loop(0, EDGES // WIDE, second_part, 0, unroll=4)
        mesh_update(state, M, sum_m, msgs[...], mw.at[layer], mg[layer, 1:2, :], turn)

    mesh_out = pltpu.make_async_copy(state, mout_h, out_sem.at[0])
    mesh_out.start()
    loaded("decw", "decg", "dedge")
    mown[2] = dot(state[...], decw[1]).astype(BF)
    rim_start(mown.at[2], mrim.at[2], RIM_M, 3)
    node[...] = dot(glat[...], decw[4])
    gown[...] = dot(glat[...], decw[2]).astype(BF)

    edge = lax.broadcasted_iota(I32, (DEC_BLOCK, NODE_BLOCK), 0) - 3 * lax.broadcasted_iota(
        I32, (DEC_BLOCK, NODE_BLOCK), 1
    )
    repeat = onehot((edge >= 0) & (edge < 3))
    edge = lax.broadcasted_iota(I32, (NODE_BLOCK, DEC_BLOCK), 1) - 3 * lax.broadcasted_iota(
        I32, (NODE_BLOCK, DEC_BLOCK), 0
    )
    gather = onehot((edge >= 0) & (edge < 3))

    def decode_first(n, _):
        rows = pl.ds(pl.multiple_of(n * DEC_BLOCK, DEC_BLOCK), DEC_BLOCK)
        nodes = pl.ds(pl.multiple_of(n * NODE_BLOCK, NODE_BLOCK), NODE_BLOCK)
        left = jnp.concatenate([dedge[rows, :], hot_d[rows, 0:M], repeat], axis=1)
        right = jnp.concatenate([decw[0], mown[2], gown[nodes, :]], axis=0)
        before[rows, :] = dot(left, right)
        return 0

    lax.fori_loop(0, DEC // DEC_BLOCK, decode_first, 0, unroll=2)
    ag_sent(LAYERS - 1)
    rim_sent(mown.at[LAYERS - 1], mrim.at[LAYERS - 1], RIM_M, LAYERS)
    rim_wait(mown.at[2], mrim.at[2], RIM_M, 3)

    def decode_second(n, _):
        rows = pl.ds(pl.multiple_of(n * DEC_BLOCK, DEC_BLOCK), DEC_BLOCK)
        nodes = pl.ds(pl.multiple_of(n * NODE_BLOCK, NODE_BLOCK), NODE_BLOCK)
        hidden = silu(before[rows, :] + dot(hot_d[rows, M:], mrim[2]))
        message = normed(dot(hidden, decw[3]), decg[0:1, :]).astype(BF)
        summed = dot(gather, message)
        mout[nodes, :] = node_update(
            glat[nodes, :], node[nodes, :], summed, decw[5], decw[6], decg[1:2, :]
        )
        return 0

    lax.fori_loop(0, DEC // DEC_BLOCK, decode_second, 0, unroll=2)
    grid_out = pltpu.make_async_copy(mout, gout_h, out_sem.at[1])
    grid_out.start()

    rim_sent(mown.at[2], mrim.at[2], RIM_M, 3)
    mesh_out.wait()
    grid_out.wait()


def hand_on(grid_in, mesh_in, grid_out, mesh_out):
    grid_out[...] = grid_in[...]
    mesh_out[...] = mesh_in[...]


def per_device(
    grid_features, mesh_latent, encode_edges, encode_senders, encode_targets,
    mesh_edges, mesh_senders, mesh_targets, decode_edges, decode_senders,
    embed_first, embed_second, embed_gain, encode_weights, encode_gains,
    mesh_weights, mesh_gains, decode_weights, decode_gains,
):
    operands = (
        jnp.swapaxes(grid_features[0, 0], 0, 1), mesh_latent[0, 0], encode_edges[0, 0],
        encode_senders[0], encode_targets[0], mesh_edges[0, 0], mesh_senders[0],
        mesh_targets[0], decode_edges[0, 0], decode_senders[0], embed_first, embed_second,
        embed_gain[None], encode_weights, encode_gains, mesh_weights, mesh_gains,
        decode_weights, decode_gains,
    )
    scratch = [pltpu.VMEM(a.shape, a.dtype) for a in operands] + [
        pltpu.VMEM((128, 128), I32),
        pltpu.VMEM((EDGES, 128), I32),
        pltpu.VMEM((ENC, M + 2 * G), BF),
        pltpu.VMEM((EDGES, 3 * M + EDGES), BF),
        pltpu.VMEM((DEC, 2 * M), BF),
        pltpu.VMEM((M, ENC), BF),
        pltpu.VMEM((M, EDGES), BF),
        pltpu.VMEM((G, L), BF),
        pltpu.VMEM((G, L), BF),
        pltpu.VMEM((8 * RIM_G, L), BF),
        pltpu.VMEM((3, M, L), BF),
        pltpu.VMEM((3, 8 * RIM_M, L), BF),
        pltpu.VMEM((LAYERS, 4, 2, 4, 4, CO, L), BF),
        pltpu.VMEM((M, L), BF),
        pltpu.VMEM((EDGES, L), F32),
        pltpu.VMEM((EDGES, L), BF),
        pltpu.VMEM((G, L), F32),
        pltpu.VMEM((M, L), BF),
        pltpu.VMEM((G, L), BF),
        pltpu.SemaphoreType.DMA((24,)),
        pltpu.SemaphoreType.DMA((2,)),
        pltpu.SemaphoreType.DMA((4, 8)),
        pltpu.SemaphoreType.DMA((4, 8)),
        pltpu.SemaphoreType.DMA((LAYERS, 48)),
        pltpu.SemaphoreType.DMA((LAYERS, 48)),
    ]
    grid_out, mesh_out = pl.pallas_call(
        kernel,
        out_shape=(
            jax.ShapeDtypeStruct((G, L), BF),
            jax.ShapeDtypeStruct((M, L), BF),
        ),
        in_specs=[pl.BlockSpec(memory_space=pl.ANY)] * len(operands),
        out_specs=(pl.BlockSpec(memory_space=pl.ANY), pl.BlockSpec(memory_space=pl.ANY)),
        scratch_shapes=scratch,
        compiler_params=pltpu.CompilerParams(
            collective_id=0, has_side_effects=True, vmem_limit_bytes=62 * 1024 * 1024
        ),
        cost_estimate=pl.CostEstimate(
            flops=60_000_000_000, bytes_accessed=21_000_000, transcendentals=4_000_000
        ),
    )(*operands)
    grid_out, mesh_out = pl.pallas_call(
        hand_on,
        out_shape=(
            jax.ShapeDtypeStruct((G, L), BF),
            jax.ShapeDtypeStruct((M, L), BF),
        ),
        in_specs=[pl.BlockSpec(memory_space=pltpu.VMEM)] * 2,
        out_specs=(pl.BlockSpec(memory_space=pltpu.VMEM), pl.BlockSpec(memory_space=pltpu.VMEM)),
    )(grid_out, mesh_out)
    return (grid_out[None, None], mesh_out[None, None])


def solution(mesh):
    block, row = P("grid", "dom", None, None), P("grid", "dom", None)
    return jax.shard_map(
        per_device,
        mesh=mesh,
        in_specs=(block, block, block, row, row, block, row, row, block, row) + (P(),) * 9,
        out_specs=(block, block),
        check_vma=False,
    )
```

```python
import jax
import jax.numpy as jnp
from jax import lax
from jax.experimental import pallas as pl
from jax.experimental.pallas import tpu as pltpu
from jax.sharding import PartitionSpec as P

L = 512
C_IN = 474
G = 512
M = 256
CO = 16
RIM_G = 64
RIM_M = 32
ENC = 1024
EDGES = 2048
DEC = 1536
LAYERS = 2
BLOCK = 256
WIDE = 512
DEC_BLOCK = 768
NODE_BLOCK = DEC_BLOCK // 3
EPS = 1e-05
MESH = pl.DeviceIdType.MESH
BF = jnp.bfloat16
F32 = jnp.float32
I32 = jnp.int32

ROW_MS, ROW_MT, ROW_DS, ROW_ES, ROW_ET = 0, 16, 32, 44, 52


def dot(a, b):
    return jnp.dot(a, b, preferred_element_type=F32)


def silu(x):
    half = 0.5 * x
    return (half + half * jnp.tanh(half)).astype(BF)


def normed(values, gain):
    centred = values - jnp.mean(values, axis=-1, keepdims=True)
    variance = jnp.mean(centred * centred, axis=-1, keepdims=True)
    return centred * lax.rsqrt(variance + EPS) * gain


def onehot(same):
    return jnp.where(same, 1.0, 0.0).astype(BF)


def kernel(
    feat_h, mlat_h, eedge_h, esnd_h, etgt_h, medge_h, msnd_h, mtgt_h, dedge_h, dsnd_h,
    ew1_h, ew2_h, eg_h, encw_h, encg_h, mw_h, mg_h, decw_h, decg_h,
    gout_h, mout_h,
    feat, mlat, eedge, esnd, etgt, medge, msnd, mtgt, dedge, dsnd,
    ew1, ew2, eg, encw, encg, mw, mg, decw, decg,
    page, wide, hot_e, hot_m, hot_d, sum_e, sum_m,
    glat, gown, grim, mown, mrim, coarse, recv, before, msgs, node, state, mout,
    in_sem, out_sem, rim_send, rim_recv, ag_send, ag_recv,
):
    band = lax.axis_index("grid")
    sector = lax.axis_index("dom")
    x, core = band // 2, band % 2
    z, y = sector // 4, sector % 4

    loads = {}

    def load(name, src, dst):
        copy = pltpu.make_async_copy(src, dst, in_sem.at[len(loads)])
        copy.start()
        loads[name] = copy

    def loaded(*names):
        for name in names:
            loads[name].wait()

    load("feat", feat_h, feat)
    load("ew1", ew1_h, ew1)
    load("ew2", ew2_h, ew2)
    load("eg", eg_h, eg)
    load("encw1", encw_h.at[pl.ds(0, 3)], encw.at[pl.ds(0, 3)])
    load("msnd", msnd_h, msnd)
    load("mtgt", mtgt_h, mtgt)
    load("dsnd", dsnd_h, dsnd)
    load("esnd", esnd_h, esnd)
    load("etgt", etgt_h, etgt)
    load("mlat", mlat_h, mlat)
    load("eedge", eedge_h, eedge)
    load("encw2", encw_h.at[pl.ds(3, 4)], encw.at[pl.ds(3, 4)])
    load("encg", encg_h, encg)
    load("mg", mg_h, mg)
    load("medge", medge_h, medge)
    load("mw0", mw_h.at[0], mw.at[0])
    load("decg", decg_h, decg)
    load("dedge", dedge_h, dedge)
    load("decw", decw_h, decw)
    load("mw1", mw_h.at[1], mw.at[1])

    def offset_of(r):
        return r // 3 - 1, r % 3 - 1

    def inside(i, j):
        row, column = band + i, sector + j
        return (row >= 0) & (row < 8) & (column >= 0) & (column < 16)

    def slot_of(r):
        return r if r < 4 else r - 1

    around = [r for r in range(9) if r != 4]

    def pick(on_zero, on_one):
        return on_zero * (1 - core) + on_one * core

    g, t = pick(z, x), pick(x, z)

    def back(value):
        return lax.rem(value + 4, 4)

    def at_core(gv, tv, yv):
        return (pick(tv, gv) * 2 + core, pick(gv, tv) * 4 + yv)

    plane = [(dg, dy) for dg in (2, 1, 3, 0) for dy in (2, 1, 3, 0) if dg + dy]
    partner = (x * 2 + 1 - core, sector)

    barrier = pltpu.get_barrier_semaphore()
    met = jnp.int32(19)
    for r in around:
        i, j = offset_of(r)
        met = met + inside(i, j).astype(I32)

        @pl.when(inside(i, j))
        def _():
            pl.semaphore_signal(barrier, inc=1, device_id=(band + i, sector + j), device_id_type=MESH)

    for dg, dy in plane:
        peer = at_core(back(g + dg), t, back(y + dy))
        pl.semaphore_signal(barrier, inc=1, device_id=peer, device_id_type=MESH)
    for k in range(1, 4):
        pl.semaphore_signal(barrier, inc=1, device_id=at_core(g, back(t + k), y), device_id_type=MESH)
    pl.semaphore_signal(barrier, inc=1, device_id=partner, device_id_type=MESH)

    def rim_copy(rows, rim, width, turn, r_to):
        i, j = offset_of(r_to)
        slot = slot_of(8 - r_to)
        first = rows.shape[0] - width if r_to > 4 else 0
        return pltpu.make_async_remote_copy(
            src_ref=rows.at[pl.ds(first, width)],
            dst_ref=rim.at[pl.ds(slot * width, width)],
            send_sem=rim_send.at[turn, slot],
            recv_sem=rim_recv.at[turn, slot],
            device_id=(band + i, sector + j),
            device_id_type=MESH,
        )

    def rim_start(rows, rim, width, turn):
        for r_to in around:
            @pl.when(inside(*offset_of(r_to)))
            def _():
                rim_copy(rows, rim, width, turn, r_to).start()

            r_from = 8 - r_to
            slot = slot_of(r_from)

            @pl.when(jnp.logical_not(inside(*offset_of(r_from))))
            def _():
                rim[pl.ds(slot * width, width), :] = jnp.zeros((width, L), BF)

    def rim_wait(rows, rim, width, turn):
        for r_from in around:
            @pl.when(inside(*offset_of(r_from)))
            def _():
                rim_copy(rows, rim, width, turn, 8 - r_from).wait_recv()

    def rim_sent(rows, rim, width, turn):
        for r_to in around:
            @pl.when(inside(*offset_of(r_to)))
            def _():
                rim_copy(rows, rim, width, turn, r_to).wait_send()

    def ag_copy(turn, piece, sem, peer):
        return pltpu.make_async_remote_copy(
            src_ref=piece,
            dst_ref=piece,
            send_sem=ag_send.at[turn, sem],
            recv_sem=ag_recv.at[turn, sem],
            device_id=peer,
            device_id_type=MESH,
        )

    def group(turn, gv, tv):
        return coarse.at[turn, pick(tv, gv), core, pick(gv, tv)]

    def plane_send(turn, dg, dy):
        piece = coarse.at[turn, x, core, z, y]
        return ag_copy(turn, piece, dg * 4 + dy, at_core(back(g + dg), t, back(y + dy)))

    def plane_come(turn, dg, dy):
        gv = back(g - dg)
        piece = coarse.at[turn, pick(t, gv), core, pick(gv, t), back(y - dy)]
        return ag_copy(turn, piece, dg * 4 + dy, partner)

    def line_send(turn, dg, k):
        return ag_copy(turn, group(turn, back(g - dg), t), 16 + dg * 4 + k, at_core(g, back(t + k), y))

    def line_come(turn, dg, k):
        return ag_copy(turn, group(turn, back(g - dg), back(t - k)), 16 + dg * 4 + k, partner)

    def core_send(turn, v):
        return ag_copy(turn, coarse.at[turn, v, core], 32 + v, partner)

    def core_come(turn, v):
        return ag_copy(turn, coarse.at[turn, v, 1 - core], 32 + v, partner)

    def ag_start(turn):
        for dg, dy in plane:
            plane_send(turn, dg, dy).start()

    def ag_second(turn):
        for dg in (0, 1, 3, 2):
            for dy in (0, 1, 3, 2):
                if dg + dy:
                    plane_come(turn, dg, dy).wait_recv()
            for k in (2, 1, 3):
                line_send(turn, dg, k).start()

    def ag_third(turn):
        for dg in (0, 1, 3, 2):
            for k in (1, 3, 2):
                line_come(turn, dg, k).wait_recv()
        for v in range(4):
            core_send(turn, v).start()

    def ag_last(turn):
        for v in range(4):
            core_come(turn, v).wait_recv()

    def ag_sent(turn):
        for dg, dy in plane:
            plane_send(turn, dg, dy).wait_send()
        for dg in range(4):
            for k in range(1, 4):
                line_send(turn, dg, k).wait_send()
            core_send(turn, dg).wait_send()

    loaded("feat", "ew1")
    hidden = silu(
        lax.dot_general(feat[...], ew1[...], (((0,), (0,)), ((), ())), preferred_element_type=F32)
    )
    loaded("ew2", "eg")
    glat[...] = normed(dot(hidden, ew2[...]), eg[...]).astype(BF)
    loaded("encw1")
    gown[...] = dot(glat[...], encw[1]).astype(BF)
    pl.semaphore_wait(barrier, met)
    rim_start(gown, grim, RIM_G, 0)

    loaded("msnd", "mtgt", "dsnd", "esnd", "etgt")
    page[...] = jnp.zeros_like(page)
    for ref, row in ((msnd, ROW_MS), (mtgt, ROW_MT), (dsnd, ROW_DS), (esnd, ROW_ES), (etgt, ROW_ET)):
        for n in range(ref.shape[1] // 128):
            page[row + n : row + n + 1, :] = ref[:, n * 128 : (n + 1) * 128]
    turned = page[...].T

    def spread(row, count):
        for n in range(count):
            wide[n * 128 : (n + 1) * 128, :] = jnp.broadcast_to(
                turned[:, row + n : row + n + 1], (128, 128)
            )

    def lanes(rows):
        return lax.broadcasted_iota(I32, (rows, 128), 1)

    def hot_columns(out, first, base, count, step):
        def body(n, _):
            rows = pl.ds(pl.multiple_of(n * step, step), step)
            values = wide[rows, :]
            ids = lanes(step)
            for t, start in enumerate(base):
                column = first + t * 128
                out[rows, column : column + 128] = onehot(values == ids + start)
            return 0

        lax.fori_loop(0, count // step, body, 0)

    def near_base(total, width):
        return [4 * total + n * 128 for n in range(total // 128)]

    def hot_rim(out, first, total, width, count, step):
        def body(n, _):
            rows = pl.ds(pl.multiple_of(n * step, step), step)
            values = wide[rows, :]
            per = 128 // width
            for t in range(8 * width // 128):
                lane = lanes(step)
                slot = t * per + lane // width
                r = jnp.where(slot < 4, slot, slot + 1)
                ids = r * total + jnp.where(slot < 4, total - width, 0) + lane % width
                column = first + t * 128
                out[rows, column : column + 128] = onehot(values == ids)
            return 0

        lax.fori_loop(0, count // step, body, 0)

    def hot_targets(out, row, count):
        for n in range(count // 128):
            ids = lax.broadcasted_iota(I32, (M, 128), 0)
            out[:, n * 128 : (n + 1) * 128] = onehot(ids == page[row + n : row + n + 1, :])

    spread(ROW_ET, ENC // 128)
    hot_columns(hot_e, 0, [0, 128], ENC, 128)
    spread(ROW_ES, ENC // 128)
    hot_columns(hot_e, M, near_base(G, RIM_G), ENC, 128)
    hot_rim(hot_e, M + G, G, RIM_G, ENC, 128)
    hot_targets(sum_e, ROW_ET, ENC)
    spread(ROW_MT, EDGES // 128)
    hot_columns(hot_m, 0, [0, 128], EDGES, 128)
    spread(ROW_MS, EDGES // 128)
    hot_columns(hot_m, M, near_base(M, RIM_M), EDGES, 128)
    hot_rim(hot_m, 2 * M, M, RIM_M, EDGES, 128)
    hot_columns(hot_m, 3 * M, [9 * M + n * 128 for n in range(16)], EDGES, 128)
    hot_targets(sum_m, ROW_MT, EDGES)
    spread(ROW_DS, DEC // 128)
    hot_columns(hot_d, 0, near_base(M, RIM_M), DEC, 128)
    hot_rim(hot_d, M, M, RIM_M, DEC, 128)

    def block_rows(n):
        return pl.ds(pl.multiple_of(n * BLOCK, BLOCK), BLOCK)

    loaded("mlat", "eedge", "encw2", "encg")
    recv[...] = dot(mlat[...], encw[2]).astype(BF)
    node[0:M, :] = dot(mlat[...], encw[4])

    def encode_first(n, _):
        rows = pl.ds(pl.multiple_of(n * WIDE, WIDE), WIDE)
        left = jnp.concatenate([eedge[rows, :], hot_e[rows, 0 : M + G]], axis=1)
        right = jnp.concatenate([encw[0], recv[...], gown[...]], axis=0)
        before[rows, :] = dot(left, right)
        return 0

    lax.fori_loop(0, ENC // WIDE, encode_first, 0, unroll=2)
    rim_wait(gown, grim, RIM_G, 0)

    def encode_second(n, _):
        rows = pl.ds(pl.multiple_of(n * WIDE, WIDE), WIDE)
        hidden = silu(before[rows, :] + dot(hot_e[rows, M + G :], grim[...]))
        msgs[rows, :] = normed(dot(hidden, encw[3]), encg[0:1, :]).astype(BF)
        return 0

    lax.fori_loop(0, ENC // WIDE, encode_second, 0, unroll=2)

    def node_update(rows_state, own_part, summed, weight_sum, weight_out, gain):
        inner = own_part + dot(summed.astype(BF), weight_sum)
        return (rows_state.astype(F32) + normed(dot(silu(inner), weight_out), gain)).astype(BF)

    def mesh_update(old, count, sums, messages, weights, gain, turn):
        def update(rows):
            summed = dot(sums[0:rows, :], messages)
            return node_update(
                old[0:rows, :], node[0:rows, :], summed, weights[5], weights[6], gain
            )

        if turn < LAYERS:
            loaded("mw0" if turn == 0 else "mw1")
            coarse[turn, x, core, z, y] = dot(update(CO), mw[turn, 1]).astype(BF)
            ag_start(turn)
        state[...] = update(count)

    mesh_update(mlat, M, sum_e, msgs[0:ENC, :], encw, encg[1:2, :], 0)

    loaded("mg", "medge")
    for layer in range(LAYERS):
        turn = layer + 1
        weights = [mw.at[layer, k] for k in range(7)]
        now = state[...]
        send = dot(now, weights[1][...]).astype(BF)
        mown[layer] = send
        recv[...] = dot(now, weights[2][...]).astype(BF)
        node[0:M, :] = dot(now, weights[4][...])

        def first_part(n, _):
            rows = pl.ds(pl.multiple_of(n * BLOCK, BLOCK), BLOCK)
            left = jnp.concatenate([medge[rows, :], hot_m[rows, 0 : 2 * M]], axis=1)
            right = jnp.concatenate([weights[0][...], recv[...], mown[layer]], axis=0)
            before[rows, :] = dot(left, right)
            return 0

        ag_second(layer)
        rim_start(mown.at[layer], mrim.at[layer], RIM_M, turn)
        lax.fori_loop(0, EDGES // BLOCK, first_part, 0, unroll=4)
        if layer == 0:
            rim_sent(gown, grim, RIM_G, 0)
        else:
            ag_sent(layer - 1)
            rim_sent(mown.at[layer - 1], mrim.at[layer - 1], RIM_M, layer)
        ag_third(layer)
        rim_wait(mown.at[layer], mrim.at[layer], RIM_M, turn)

        def half(rows, on):
            columns = [
                hot_m[rows, pl.ds(pl.multiple_of((3 + 2 * v + on) * M, M), M)] for v in range(4)
            ]
            table = [coarse[layer, v, on].reshape(16 * CO, L) for v in range(4)]
            return columns, table

        def own_half(n, _):
            rows = pl.ds(pl.multiple_of(n * WIDE, WIDE), WIDE)
            columns, table = half(rows, core)
            left = jnp.concatenate([hot_m[rows, 2 * M : 3 * M]] + columns, axis=1)
            before[rows, :] += dot(left, jnp.concatenate([mrim[layer]] + table, axis=0))
            return 0

        lax.fori_loop(0, EDGES // WIDE, own_half, 0, unroll=2)
        ag_last(layer)

        def second_part(n, _):
            rows = pl.ds(pl.multiple_of(n * WIDE, WIDE), WIDE)
            columns, table = half(rows, 1 - core)
            left, right = jnp.concatenate(columns, axis=1), jnp.concatenate(table, axis=0)
            hidden = silu(before[rows, :] + dot(left, right))
            message = normed(dot(hidden, weights[3][...]), mg[layer, 0:1, :])
            if layer + 1 < LAYERS:
                medge[rows, :] = (medge[rows, :].astype(F32) + message).astype(BF)
            msgs[rows, :] = message.astype(BF)
            return 0

        lax.fori_loop(0, EDGES // WIDE, second_part, 0, unroll=4)
        mesh_update(state, M, sum_m, msgs[...], mw.at[layer], mg[layer, 1:2, :], turn)

    mesh_out = pltpu.make_async_copy(state, mout_h, out_sem.at[0])
    mesh_out.start()
    loaded("decw", "decg", "dedge")
    mown[2] = dot(state[...], decw[1]).astype(BF)
    rim_start(mown.at[2], mrim.at[2], RIM_M, 3)
    node[...] = dot(glat[...], decw[4])
    gown[...] = dot(glat[...], decw[2]).astype(BF)

    edge = lax.broadcasted_iota(I32, (DEC_BLOCK, NODE_BLOCK), 0) - 3 * lax.broadcasted_iota(
        I32, (DEC_BLOCK, NODE_BLOCK), 1
    )
    repeat = onehot((edge >= 0) & (edge < 3))
    edge = lax.broadcasted_iota(I32, (NODE_BLOCK, DEC_BLOCK), 1) - 3 * lax.broadcasted_iota(
        I32, (NODE_BLOCK, DEC_BLOCK), 0
    )
    gather = onehot((edge >= 0) & (edge < 3))

    def decode_first(n, _):
        rows = pl.ds(pl.multiple_of(n * DEC_BLOCK, DEC_BLOCK), DEC_BLOCK)
        nodes = pl.ds(pl.multiple_of(n * NODE_BLOCK, NODE_BLOCK), NODE_BLOCK)
        left = jnp.concatenate([dedge[rows, :], hot_d[rows, 0:M], repeat], axis=1)
        right = jnp.concatenate([decw[0], mown[2], gown[nodes, :]], axis=0)
        before[rows, :] = dot(left, right)
        return 0

    lax.fori_loop(0, DEC // DEC_BLOCK, decode_first, 0, unroll=2)
    ag_sent(LAYERS - 1)
    rim_sent(mown.at[LAYERS - 1], mrim.at[LAYERS - 1], RIM_M, LAYERS)
    rim_wait(mown.at[2], mrim.at[2], RIM_M, 3)

    def decode_second(n, _):
        rows = pl.ds(pl.multiple_of(n * DEC_BLOCK, DEC_BLOCK), DEC_BLOCK)
        nodes = pl.ds(pl.multiple_of(n * NODE_BLOCK, NODE_BLOCK), NODE_BLOCK)
        hidden = silu(before[rows, :] + dot(hot_d[rows, M:], mrim[2]))
        message = normed(dot(hidden, decw[3]), decg[0:1, :]).astype(BF)
        summed = dot(gather, message)
        mout[nodes, :] = node_update(
            glat[nodes, :], node[nodes, :], summed, decw[5], decw[6], decg[1:2, :]
        )
        return 0

    lax.fori_loop(0, DEC // DEC_BLOCK, decode_second, 0, unroll=2)
    grid_out = pltpu.make_async_copy(mout, gout_h, out_sem.at[1])
    grid_out.start()

    rim_sent(mown.at[2], mrim.at[2], RIM_M, 3)
    mesh_out.wait()
    grid_out.wait()


def hand_on(grid_in, mesh_in, grid_out, mesh_out):
    grid_out[...] = grid_in[...]
    mesh_out[...] = mesh_in[...]


def per_device(
    grid_features, mesh_latent, encode_edges, encode_senders, encode_targets,
    mesh_edges, mesh_senders, mesh_targets, decode_edges, decode_senders,
    embed_first, embed_second, embed_gain, encode_weights, encode_gains,
    mesh_weights, mesh_gains, decode_weights, decode_gains,
):
    operands = (
        jnp.swapaxes(grid_features[0, 0], 0, 1), mesh_latent[0, 0], encode_edges[0, 0],
        encode_senders[0], encode_targets[0], mesh_edges[0, 0], mesh_senders[0],
        mesh_targets[0], decode_edges[0, 0], decode_senders[0], embed_first, embed_second,
        embed_gain[None], encode_weights, encode_gains, mesh_weights, mesh_gains,
        decode_weights, decode_gains,
    )
    scratch = [pltpu.VMEM(a.shape, a.dtype) for a in operands] + [
        pltpu.VMEM((128, 128), I32),
        pltpu.VMEM((EDGES, 128), I32),
        pltpu.VMEM((ENC, M + 2 * G), BF),
        pltpu.VMEM((EDGES, 3 * M + EDGES), BF),
        pltpu.VMEM((DEC, 2 * M), BF),
        pltpu.VMEM((M, ENC), BF),
        pltpu.VMEM((M, EDGES), BF),
        pltpu.VMEM((G, L), BF),
        pltpu.VMEM((G, L), BF),
        pltpu.VMEM((8 * RIM_G, L), BF),
        pltpu.VMEM((3, M, L), BF),
        pltpu.VMEM((3, 8 * RIM_M, L), BF),
        pltpu.VMEM((LAYERS, 4, 2, 4, 4, CO, L), BF),
        pltpu.VMEM((M, L), BF),
        pltpu.VMEM((EDGES, L), F32),
        pltpu.VMEM((EDGES, L), BF),
        pltpu.VMEM((G, L), F32),
        pltpu.VMEM((M, L), BF),
        pltpu.VMEM((G, L), BF),
        pltpu.SemaphoreType.DMA((24,)),
        pltpu.SemaphoreType.DMA((2,)),
        pltpu.SemaphoreType.DMA((4, 8)),
        pltpu.SemaphoreType.DMA((4, 8)),
        pltpu.SemaphoreType.DMA((LAYERS, 36)),
        pltpu.SemaphoreType.DMA((LAYERS, 36)),
    ]
    grid_out, mesh_out = pl.pallas_call(
        kernel,
        out_shape=(
            jax.ShapeDtypeStruct((G, L), BF),
            jax.ShapeDtypeStruct((M, L), BF),
        ),
        in_specs=[pl.BlockSpec(memory_space=pl.ANY)] * len(operands),
        out_specs=(pl.BlockSpec(memory_space=pl.ANY), pl.BlockSpec(memory_space=pl.ANY)),
        scratch_shapes=scratch,
        compiler_params=pltpu.CompilerParams(
            collective_id=0, has_side_effects=True, vmem_limit_bytes=62 * 1024 * 1024
        ),
        cost_estimate=pl.CostEstimate(
            flops=60_000_000_000, bytes_accessed=21_000_000, transcendentals=4_000_000
        ),
    )(*operands)
    grid_out, mesh_out = pl.pallas_call(
        hand_on,
        out_shape=(
            jax.ShapeDtypeStruct((G, L), BF),
            jax.ShapeDtypeStruct((M, L), BF),
        ),
        in_specs=[pl.BlockSpec(memory_space=pltpu.VMEM)] * 2,
        out_specs=(pl.BlockSpec(memory_space=pltpu.VMEM), pl.BlockSpec(memory_space=pltpu.VMEM)),
    )(grid_out, mesh_out)
    return (grid_out[None, None], mesh_out[None, None])


def solution(mesh):
    block, row = P("grid", "dom", None, None), P("grid", "dom", None)
    return jax.shard_map(
        per_device,
        mesh=mesh,
        in_specs=(block, block, block, row, row, block, row, row, block, row) + (P(),) * 9,
        out_specs=(block, block),
        check_vma=False,
    )
```
